32 devices in a mesh: lat: 4 (over y, x), lon: 8 (over z, core).
Axes of the slice: x: 2, y: 2, z: 4, core: 2. Of those that a mesh axis runs over, the one named last changes fastest.
Arguments:
- query_tok: bfloat16 [32, 128, 1536], P('lat', 'lon'), may hold values from -9 to 9
- key_tok: bfloat16 [32, 128, 1536], P('lat', 'lon'), may hold values from -9 to 9
- value_tok: bfloat16 [32, 128, 1536], P('lat', 'lon'), may hold values from -6 to 6
- query_tan: bfloat16 [32, 128, 1536], P('lat', 'lon'), may hold values from -6 to 6
- key_tan: bfloat16 [32, 128, 1536], P('lat', 'lon'), may hold values from -6 to 6
- value_tan: bfloat16 [32, 128, 1536], P('lat', 'lon'), may hold values from -6 to 6
Outputs:
- attended: bfloat16 [32, 128, 1536], P('lat', 'lon')
- attended_tan: bfloat16 [32, 128, 1536], P('lat', 'lon')
The draws below stay inside these ranges and needn't reach their ends.
All inputs are finite; a program needn't handle non-finite values.
Results may differ from the reference program's by a relative error of at most 0.012.
The reference program's roundings to bfloat16 on the way count: a program that leaves them out, or rounds other values in their place, can miss the bound.
Values may be sent and summed in bfloat16 or wider, within the bound.
A program may use at most 64 MiB of HBM per device.

```python
import math
import jax
import jax.numpy as jnp
from jax import lax

HEADS = 12
HD = 128
WIN = 16
NH = 32
NW = 128


def drawn_pair(key):
    base_key = jax.random.fold_in(key, 7)
    shape_all = (NH, NW, HEADS * HD)
    query_part = jnp.clip(jax.random.normal(jax.random.fold_in(base_key, 1), shape_all, jnp.float32), -6.0, 6.0)
    key_part = jnp.clip(jax.random.normal(jax.random.fold_in(base_key, 2), shape_all, jnp.float32), -6.0, 6.0)
    return (query_part, key_part)


def draw_query_tok(key, part):
    return drawn_pair(key)[0].astype(jnp.bfloat16)


def draw_key_tok(key, part):
    return drawn_pair(key)[1].astype(jnp.bfloat16)


def shard_levels(key, dims, shards, low, largest):
    def one(axis_at, parts):
        steps = jax.random.uniform(jax.random.fold_in(jax.random.fold_in(key, 6), axis_at), (parts,), jnp.float32, low / len(shards), largest / len(shards))
        return jnp.repeat(jnp.exp(steps), dims[axis_at] // parts).reshape((-1,) + (1,) * (len(dims) - axis_at - 1))

    factor_of = one(*shards[0])
    for cut in shards[1:]:
        factor_of = factor_of * one(*cut)
    return factor_of


def noise(own_key, dims, width, reach, split=(), kind=jnp.bfloat16):
    result = width * jax.random.normal(own_key, dims, jnp.float32)
    if split:
        result = result * shard_levels(own_key, dims, split, -0.22, 0.18)
    return jnp.clip(result, -reach, reach).astype(kind)


def setup_inputs(seed: int = 0) -> dict:
    key_list = jax.random.split(jax.random.key(seed), 7)
    query_tok = draw_query_tok(jax.random.fold_in(key_list[6], 71), 0)
    key_tok = draw_key_tok(jax.random.fold_in(key_list[6], 71), 0)
    value_tok = noise(key_list[2], (NH, NW, HEADS * HD), 1.0, 6.0, ((0, 4), (1, 8)))
    query_tan = noise(key_list[3], (NH, NW, HEADS * HD), 1.0, 6.0, ((0, 4), (1, 8)))
    key_tan = noise(key_list[4], (NH, NW, HEADS * HD), 1.0, 6.0, ((0, 4), (1, 8)))
    value_tan = noise(key_list[5], (NH, NW, HEADS * HD), 1.0, 6.0, ((0, 4), (1, 8)))
    return {"query_tok": query_tok, "key_tok": key_tok, "value_tok": value_tok, "query_tan": query_tan, "key_tan": key_tan, "value_tan": value_tan}


def rotate_rays(values, row_first, col_first, total_rows, total_cols):
    band_rows, sector_cols, feature_width = values.shape
    quarter = HD // 4
    head_count = feature_width // HD
    frequency = (jnp.arange(quarter, dtype=jnp.int32) + 1).astype(jnp.float32)
    row_ids = (row_first + jnp.arange(band_rows, dtype=jnp.int32)).astype(jnp.float32)
    col_ids = (col_first + jnp.arange(sector_cols, dtype=jnp.int32)).astype(jnp.float32)
    lat_angle = ((row_ids + 0.5) * (math.pi / total_rows))[:, None] * frequency[None, :]
    lon_angle = (col_ids * (2.0 * math.pi / total_cols))[:, None] * frequency[None, :]
    lat_cos = jnp.cos(lat_angle)[:, None, None, :]
    lat_sin = jnp.sin(lat_angle)[:, None, None, :]
    lon_cos = jnp.cos(lon_angle)[None, :, None, :]
    lon_sin = jnp.sin(lon_angle)[None, :, None, :]
    quarters = values.astype(jnp.float32).reshape(band_rows, sector_cols, head_count, 4, quarter)
    lat_one = quarters[:, :, :, 0, :]
    lat_two = quarters[:, :, :, 1, :]
    lon_one = quarters[:, :, :, 2, :]
    lon_two = quarters[:, :, :, 3, :]
    turned = jnp.stack([lat_one * lat_cos - lat_two * lat_sin, lat_one * lat_sin + lat_two * lat_cos, lon_one * lon_cos - lon_two * lon_sin, lon_one * lon_sin + lon_two * lon_cos], axis=3)
    return turned.reshape(band_rows, sector_cols, feature_width).astype(jnp.bfloat16)

def reference(query_tok, key_tok, value_tok, query_tan, key_tan, value_tan):
    radius = WIN // 2
    window_span = 2 * radius
    score_scale = 1.0 / math.sqrt(HD)
    rot_query = rotate_rays(query_tok, 0, 0, NH, NW)
    rot_qtan = rotate_rays(query_tan, 0, 0, NH, NW)
    rot_key = rotate_rays(key_tok, 0, 0, NH, NW)
    rot_ktan = rotate_rays(key_tan, 0, 0, NH, NW)

    def widen(source):
        wrapped = jnp.concatenate([source[:, NW - radius:], source, source[:, :radius - 1]], axis=1)
        padded = jnp.pad(wrapped, ((radius, radius - 1), (0, 0), (0, 0)))
        return padded.reshape(NH + window_span - 1, NW + window_span - 1, HEADS, HD)
    key_wide = widen(rot_key)
    ktan_wide = widen(rot_ktan)
    value_wide = widen(value_tok)
    vtan_wide = widen(value_tan)
    row_ids = jnp.arange(NH + window_span - 1, dtype=jnp.int32) - radius
    row_valid = (row_ids >= 0) & (row_ids < NH)

    def one_row(row_index):
        q_row = rot_query[row_index].reshape(NW, HEADS, HD).astype(jnp.float32)
        qt_row = rot_qtan[row_index].reshape(NW, HEADS, HD).astype(jnp.float32)

        def band_of(source):
            return lax.dynamic_slice_in_dim(source, row_index, window_span, 0).astype(jnp.float32)
        k_band = band_of(key_wide)
        kt_band = band_of(ktan_wide)
        v_band = band_of(value_wide)
        vt_band = band_of(vtan_wide)
        valid_band = lax.dynamic_slice_in_dim(row_valid, row_index, window_span, 0)
        score_list = []
        slope_list = []
        for offset in range(window_span):
            k_cols = k_band[:, offset:offset + NW]
            kt_cols = kt_band[:, offset:offset + NW]
            score_list.append(jnp.einsum('chd,ychd->chy', q_row, k_cols) * score_scale)
            slope_list.append((jnp.einsum('chd,ychd->chy', qt_row, k_cols) + jnp.einsum('chd,ychd->chy', q_row, kt_cols)) * score_scale)
        scores = jnp.stack(score_list, axis=-1)
        slopes = jnp.stack(slope_list, axis=-1)
        scores = jnp.where(valid_band[None, None, :, None], scores, -1e+30)
        row_top = lax.optimization_barrier(jnp.max(scores, axis=(2, 3), keepdims=True))
        exp_scores = jnp.exp(scores - row_top)
        attention = exp_scores / lax.optimization_barrier(jnp.sum(exp_scores, axis=(2, 3), keepdims=True))
        mean_slope = lax.optimization_barrier(jnp.sum(attention * slopes, axis=(2, 3), keepdims=True))
        weight_b = (attention * (slopes - mean_slope)).astype(jnp.bfloat16)
        prob_b = attention.astype(jnp.bfloat16)
        total_out = jnp.zeros((NW, HEADS, HD), jnp.float32)
        total_tan = jnp.zeros((NW, HEADS, HD), jnp.float32)
        for offset in range(window_span):
            v_cols = v_band[:, offset:offset + NW]
            vt_cols = vt_band[:, offset:offset + NW]
            prob_here = prob_b[..., offset].astype(jnp.float32)
            weight_here = weight_b[..., offset].astype(jnp.float32)
            total_out = total_out + jnp.einsum('chy,ychd->chd', prob_here, v_cols)
            total_tan = total_tan + jnp.einsum('chy,ychd->chd', weight_here, v_cols) + jnp.einsum('chy,ychd->chd', prob_here, vt_cols)
        return (total_out.reshape(NW, HEADS * HD).astype(jnp.bfloat16), total_tan.reshape(NW, HEADS * HD).astype(jnp.bfloat16))
    results = lax.map(one_row, jnp.arange(NH, dtype=jnp.int32))
    return (results[0], results[1])
```

```python
import functools
import math

import jax
import jax.numpy as jnp
import numpy as np
from jax import lax
from jax.experimental import pallas as pl
from jax.experimental.pallas import tpu as pltpu
from jax.sharding import PartitionSpec as P

HD = 128
WIN = 16


def extended_2(shard, sides, width, wrap):
    for axis, dim in sides:
        count, length = (lax.axis_size(axis), shard.shape[dim])
        up = [(i, (i + 1) % count) for i in range(count if wrap else count - 1)]
        down = [(j, i) for i, j in up]
        last = lax.slice_in_dim(shard, length - width, length, axis=dim)
        leading = lax.slice_in_dim(shard, 0, width, axis=dim)
        before = lax.ppermute(last, axis, up)
        after = lax.ppermute(leading, axis, down)
        shard = jnp.concatenate([before, shard, after], axis=dim)
    return shard


def rotate_rays(values, row_first, col_first, total_rows, total_cols):
    band_rows, sector_cols, feature_width = values.shape
    quarter = HD // 4
    head_count = feature_width // HD
    frequency = (jnp.arange(quarter, dtype=jnp.int32) + 1).astype(jnp.float32)
    row_ids = (row_first + jnp.arange(band_rows, dtype=jnp.int32)).astype(jnp.float32)
    col_ids = (col_first + jnp.arange(sector_cols, dtype=jnp.int32)).astype(jnp.float32)
    lat_angle = ((row_ids + 0.5) * (math.pi / total_rows))[:, None] * frequency[None, :]
    lon_angle = (col_ids * (2.0 * math.pi / total_cols))[:, None] * frequency[None, :]
    lat_cos = jnp.cos(lat_angle)[:, None, None, :]
    lat_sin = jnp.sin(lat_angle)[:, None, None, :]
    lon_cos = jnp.cos(lon_angle)[None, :, None, :]
    lon_sin = jnp.sin(lon_angle)[None, :, None, :]
    quarters = values.astype(jnp.float32).reshape(band_rows, sector_cols, head_count, 4, quarter)
    lat_one = quarters[:, :, :, 0, :]
    lat_two = quarters[:, :, :, 1, :]
    lon_one = quarters[:, :, :, 2, :]
    lon_two = quarters[:, :, :, 3, :]
    turned = jnp.stack(
        [
            lat_one * lat_cos - lat_two * lat_sin,
            lat_one * lat_sin + lat_two * lat_cos,
            lon_one * lon_cos - lon_two * lon_sin,
            lon_one * lon_sin + lon_two * lon_cos,
        ],
        axis=3,
    )
    return turned.reshape(band_rows, sector_cols, feature_width).astype(jnp.bfloat16)


def widen_rows(stacked, radius):
    padded = extended_2(stacked, (("lat", 1),), radius, False)
    return padded[:, : padded.shape[1] - 1]


def widen_cols(stacked, radius):
    padded = extended_2(stacked, (("lon", 2),), radius, True)
    return padded[:, :, : padded.shape[2] - 1]


def shards_halo(query_tok, key_tok, value_tok, query_tan, key_tan, value_tan):
    band_rows, sector_cols, feature_width = query_tok.shape
    radius = WIN // 2
    window_span = 2 * radius
    score_scale = 1.0 / math.sqrt(HD)
    total_rows = band_rows * lax.axis_size("lat")
    total_cols = sector_cols * lax.axis_size("lon")
    row_first = lax.axis_index("lat") * band_rows
    col_first = lax.axis_index("lon") * sector_cols
    rot_query = rotate_rays(query_tok, row_first, col_first, total_rows, total_cols)
    rot_qtan = rotate_rays(query_tan, row_first, col_first, total_rows, total_cols)
    rot_key = rotate_rays(key_tok, row_first, col_first, total_rows, total_cols)
    rot_ktan = rotate_rays(key_tan, row_first, col_first, total_rows, total_cols)
    stacked = jnp.stack([rot_key, rot_ktan, value_tok, value_tan])
    extended = widen_rows(widen_cols(stacked, radius), radius)
    ext_rows = band_rows + window_span - 1
    ext_cols = sector_cols + window_span - 1
    key_count = ext_rows * ext_cols
    query_count = band_rows * sector_cols
    keys_flat = extended.reshape(4, key_count, feature_width)
    query_flat = rot_query.reshape(query_count, feature_width)
    qtan_flat = rot_qtan.reshape(query_count, feature_width)
    key_ids = jnp.arange(key_count, dtype=jnp.int32)
    query_ids = jnp.arange(query_count, dtype=jnp.int32)
    row_gap = (key_ids // ext_cols)[None, :] - (query_ids // sector_cols)[:, None]
    col_gap = (key_ids % ext_cols)[None, :] - (query_ids % sector_cols)[:, None]
    key_rows = row_first - radius + key_ids // ext_cols
    allowed = (
        (row_gap >= 0)
        & (row_gap < window_span)
        & (col_gap >= 0)
        & (col_gap < window_span)
        & ((key_rows >= 0) & (key_rows < total_rows))[None, :]
    )
    head_count = feature_width // HD
    group_size = math.gcd(head_count, 4)
    out_groups = []
    tan_groups = []
    for group_index in range(head_count // group_size):
        low_col = group_index * group_size * HD
        high_col = low_col + group_size * HD
        q_part = query_flat[:, low_col:high_col].reshape(query_count, group_size, HD)
        qt_part = qtan_flat[:, low_col:high_col].reshape(query_count, group_size, HD)
        k_part = keys_flat[0][:, low_col:high_col].reshape(key_count, group_size, HD)
        kt_part = keys_flat[1][:, low_col:high_col].reshape(key_count, group_size, HD)
        v_part = keys_flat[2][:, low_col:high_col].reshape(key_count, group_size, HD)
        vt_part = keys_flat[3][:, low_col:high_col].reshape(key_count, group_size, HD)
        scores = (
            jnp.einsum("qhd,khd->hqk", q_part, k_part, preferred_element_type=jnp.float32)
            * score_scale
        )
        scores = jnp.where(allowed[None], scores, -1e30)
        row_top = jnp.max(scores, axis=-1, keepdims=True)
        exp_scores = jnp.exp(scores - row_top)
        attention = exp_scores / jnp.sum(exp_scores, axis=-1, keepdims=True)
        slopes = (
            jnp.einsum("qhd,khd->hqk", qt_part, k_part, preferred_element_type=jnp.float32)
            + jnp.einsum("qhd,khd->hqk", q_part, kt_part, preferred_element_type=jnp.float32)
        ) * score_scale
        mean_slope = jnp.sum(attention * slopes, axis=-1, keepdims=True)
        weight_b = (attention * (slopes - mean_slope)).astype(jnp.bfloat16)
        prob_b = attention.astype(jnp.bfloat16)
        group_out = jnp.einsum("hqk,khd->qhd", prob_b, v_part, preferred_element_type=jnp.float32)
        group_tan = jnp.einsum(
            "hqk,khd->qhd", weight_b, v_part, preferred_element_type=jnp.float32
        ) + jnp.einsum("hqk,khd->qhd", prob_b, vt_part, preferred_element_type=jnp.float32)
        out_groups.append(group_out.reshape(query_count, group_size * HD))
        tan_groups.append(group_tan.reshape(query_count, group_size * HD))
    attended = jnp.concatenate(out_groups, axis=1).astype(jnp.bfloat16)
    attended_tan = jnp.concatenate(tan_groups, axis=1).astype(jnp.bfloat16)
    return (
        attended.reshape(band_rows, sector_cols, feature_width),
        attended_tan.reshape(band_rows, sector_cols, feature_width),
    )


BF = jnp.bfloat16
F32 = jnp.float32
MESH = pl.DeviceIdType.MESH


def ray_tables(total_rows, total_cols):
    quarter = HD // 4
    freq = (np.arange(quarter) + 1).astype(np.float32)
    rows = np.arange(total_rows).astype(np.float32)
    cols = np.arange(total_cols).astype(np.float32)
    lat = ((rows + np.float32(0.5)) * np.float32(math.pi / total_rows))[:, None] * freq[None, :]
    lon = (cols * np.float32(2.0 * math.pi / total_cols))[:, None] * freq[None, :]

    def table(fn, angle, first):
        part = fn(angle.astype(np.float64)).astype(np.float32)
        none = np.zeros_like(part)
        return np.concatenate([part, part, none, none] if first else [none, none, part, part], axis=1)

    row_tab = np.stack([table(np.cos, lat, True), table(np.sin, lat, True)])
    col_tab = np.stack([table(np.cos, lon, False), table(np.sin, lon, False)])
    return row_tab, col_tab


def kernel(
    n, n_lon, hp, band,
    q_ref, k_ref, v_ref, qt_ref, kt_ref, vt_ref, row_hbm, col_hbm,
    both_ref,
    raw_kv, raw_q, kvb, hs, outs, turn, bias, row_tab, col_tab,
    kv_send, kv_recv, q_send, q_recv, in_loc, q_loc, h_send, h_recv, o_send, o_recv, o_loc, t_loc, greet,
):
    me = lax.axis_index("lat")
    lon = lax.axis_index("lon")
    left = lax.rem(lon + n_lon - 1, n_lon)
    right = lax.rem(lon + 1, n_lon)
    cols = 16
    total = n * band
    pairs = total // 2

    barrier = pltpu.get_barrier_semaphore()
    for d in range(1, n):
        pl.semaphore_signal(barrier, inc=1, device_id=(lax.rem(me + d, n), lon), device_id_type=MESH)

    def tell(sem, side):
        pl.semaphore_signal(sem, inc=1, device_id=(me, side), device_id_type=MESH)

    first, last = lon == 0, lon == n_lon - 1
    odd = lax.rem(lon, 2) == 1
    middle_odd = jnp.logical_and(odd, jnp.logical_not(last))
    middle_even = jnp.logical_and(jnp.logical_not(odd), jnp.logical_not(first))

    @pl.when(middle_odd)
    def _():
        tell(barrier, left)
        tell(barrier, right)
        pl.semaphore_wait(barrier, n - 1)

    @pl.when(middle_even)
    def _():
        pl.semaphore_wait(barrier, n + 1)
        tell(greet, left)
        tell(greet, right)

    @pl.when(first)
    def _():
        tell(barrier, left)
        pl.semaphore_wait(barrier, n)
        tell(greet, right)

    @pl.when(last)
    def _():
        tell(barrier, left)
        pl.semaphore_wait(barrier, n)
        tell(greet, right)

    kv_refs = (k_ref, kt_ref, v_ref, vt_ref)
    q_refs = (q_ref, qt_ref)
    parts = ((0, 1), (1, hp - 1)) if hp > 1 else ((0, 1),)

    def lanes(owner, j, count):
        return pl.ds(pl.multiple_of((owner * hp + j) * HD, HD), count * HD)

    def kv_copy(a, p, d):
        peer = lax.rem(me + d, n)
        j, count = parts[p]
        return pltpu.make_async_remote_copy(
            src_ref=kv_refs[a].at[:, :, lanes(peer, j, count)],
            dst_ref=raw_kv.at[a, pl.ds(me * band, band), :, j * HD:(j + count) * HD],
            send_sem=kv_send.at[a, p, d - 1],
            recv_sem=kv_recv.at[a, p, d - 1],
            device_id=(peer, lon),
            device_id_type=MESH,
        )

    def q_copy(a, j, d):
        peer = lax.rem(me + d, n)
        return pltpu.make_async_remote_copy(
            src_ref=q_refs[a].at[:, :, lanes(peer, j, 1)],
            dst_ref=raw_q.at[j, a, pl.ds(me * band, band)],
            send_sem=q_send.at[j, a, d - 1],
            recv_sem=q_recv.at[j, a, d - 1],
            device_id=(peer, lon),
            device_id_type=MESH,
        )

    def own_q(a, j):
        return pltpu.make_async_copy(
            q_refs[a].at[:, :, lanes(me, j, 1)],
            raw_q.at[j, a, pl.ds(me * band, band)],
            q_loc.at[j, a],
        )

    def own_copy(a, p):
        j, count = parts[p]
        return pltpu.make_async_copy(
            kv_refs[a].at[:, :, lanes(me, j, count)],
            raw_kv.at[a, pl.ds(me * band, band), :, j * HD:(j + count) * HD],
            in_loc.at[a, p],
        )

    halos = [(0, slice(0, 4))] + [(p, slice(a, a + 1)) for p in range(1, len(parts)) for a in range(4)]

    def halo_copy(side, h):
        p, arrays = halos[h]
        j, count = parts[p]
        return pltpu.make_async_remote_copy(
            src_ref=hs.at[side, arrays, j:j + count],
            dst_ref=kvb.at[arrays, j:j + count, :, 3 - side],
            send_sem=h_send.at[h, side],
            recv_sem=h_recv.at[h, side],
            device_id=(me, right if side else left),
            device_id_type=MESH,
        )

    def out_copy(j, d):
        peer = lax.rem(me + d, n)
        return pltpu.make_async_remote_copy(
            src_ref=outs.at[j, :, pl.ds(peer * band, band)],
            dst_ref=both_ref.at[:, :, :, lanes(me, j, 1)],
            send_sem=o_send.at[j, d - 1],
            recv_sem=o_recv.at[j, d - 1],
            device_id=(peer, lon),
            device_id_type=MESH,
        )

    def own_out(j):
        return pltpu.make_async_copy(
            outs.at[j, :, pl.ds(me * band, band)],
            both_ref.at[:, :, :, lanes(me, j, 1)],
            o_loc.at[j],
        )

    here = pl.ds(pl.multiple_of(lon * cols, cols), cols)
    row_copy = pltpu.make_async_copy(row_hbm, row_tab, t_loc.at[0])
    col_copy = pltpu.make_async_copy(col_hbm.at[:, here], col_tab, t_loc.at[1])
    row_copy.start()
    col_copy.start()
    for p in range(len(parts)):
        for a in range(4):
            for d in range(1, n):
                kv_copy(a, p, d).start()
        for a in range(4):
            own_copy(a, p).start()
    for j in range(hp):
        for a in range(2):
            for d in range(1, n):
                q_copy(a, j, d).start()
        for a in range(2):
            own_q(a, j).start()

    row_copy.wait()
    col_copy.wait()
    for t in range(2):
        whole = row_tab[t][:, None, :] + col_tab[t][None, :, :]
        turn[t] = whole.reshape(total * cols, HD)
    shape = (band * cols, (band + WIN) * 2 * cols)
    query = lax.broadcasted_iota(jnp.int32, shape, 0)
    key = lax.broadcasted_iota(jnp.int32, shape, 1)
    part = (key % 64) // 16
    spot = key % 16
    own = part < 2
    key_row = (key // 64) * 2 + jnp.where(own, part, spot // 8)
    key_col = jnp.where(own, spot, jnp.where(part == 2, spot % 8 - 8, spot % 8 + 16))
    row_gap = key_row - query // 16
    col_gap = key_col - query % 16 + WIN // 2
    allowed = (row_gap >= 0) & (row_gap < WIN) & (col_gap >= 0) & (col_gap < WIN)
    bias[...] = jnp.where(allowed, 0.0, -1e30)
    src = lax.broadcasted_iota(jnp.int32, (HD, HD), 0)
    dst = lax.broadcasted_iota(jnp.int32, (HD, HD), 1)
    low = (dst % 64) < 32
    swap = (
        jnp.where(low & (src == dst + 32), -1.0, 0.0)
        + jnp.where(jnp.logical_not(low) & (src == dst - 32), 1.0, 0.0)
    ).astype(BF)

    def turned(x):
        flat = x.reshape(total * cols, HD)
        other = jnp.dot(flat, swap, preferred_element_type=F32)
        return flat.astype(F32) * turn[0] + other * turn[1]

    def stage(a, j):
        x = raw_kv[a, :, :, pl.ds(pl.multiple_of(j * HD, HD), HD)]
        y = turned(x) if a < 2 else x.reshape(total * cols, HD).astype(F32)
        kvb[a, j, :, 0:2] = y.reshape(pairs, 2, cols, HD).astype(BF)
        halves = y.reshape(total, 2, cols // 2, HD)
        for side in range(2):
            hs[side, a, j] = halves[:, side].reshape(pairs, cols, HD).astype(BF)

    @pl.when(middle_odd)
    def _():
        pl.semaphore_wait(greet, 2)

    @pl.when(jnp.logical_or(first, last))
    def _():
        pl.semaphore_wait(greet, 1)

    for p in range(len(parts)):
        for a in range(4):
            own_copy(a, p).wait()
            for d in range(1, n):
                kv_copy(a, p, d).wait_recv()
            if parts[p][1] == 1:
                stage(a, parts[p][0])
            else:
                pl.loop(parts[p][0], sum(parts[p]))(functools.partial(stage, a))
            for h in range(len(halos)):
                if halos[h][0] == p and halos[h][1].stop == a + 1:
                    for side in range(2):
                        halo_copy(side, h).start()

    scale2 = math.log2(math.e) / math.sqrt(HD)
    scale = 1.0 / math.sqrt(HD)

    @pl.loop(0, hp)
    def _(j):
        for p in range(len(parts)):
            @pl.when(j == parts[p][0])
            def _():
                for h in range(len(halos)):
                    if halos[h][0] == p:
                        for side in range(2):
                            halo_copy(side, h).wait_recv()

        for a in range(2):
            own_q(a, j).wait()
            for d in range(1, n):
                q_copy(a, j, d).wait_recv()
            raw_q[j, a] = turned(raw_q[j, a]).astype(BF).reshape(total, cols, HD)
        nq = band * cols
        for b in range(n):
            first = max(0, b * band - WIN // 2)
            last = min(total, (b + 1) * band + WIN // 2)
            skip = (first - (b * band - WIN // 2)) // 2 * 64
            p0, p1 = first // 2, last // 2
            nk = (p1 - p0) * 64
            keys = kvb[0, j, p0:p1].reshape(nk, HD)
            ktan = kvb[1, j, p0:p1].reshape(nk, HD)
            val = kvb[2, j, p0:p1].reshape(nk, HD)
            vtan = kvb[3, j, p0:p1].reshape(nk, HD)
            rows = slice(b * band, (b + 1) * band)
            q = raw_q[j, 0, rows].reshape(nq, HD)
            qt = raw_q[j, 1, rows].reshape(nq, HD)
            nt = (((1,), (1,)), ((), ()))
            score = lax.dot_general(q, keys, nt, preferred_element_type=F32)
            score = score * scale2 + bias[:, skip:skip + nk]
            top = jnp.max(score, axis=-1, keepdims=True)
            e = jnp.exp2(score - top)
            inv = 1.0 / jnp.sum(e, axis=-1, keepdims=True)
            slope = lax.dot_general(
                jnp.concatenate([qt, q], axis=1),
                jnp.concatenate([keys, ktan], axis=1),
                nt,
                preferred_element_type=F32,
            )
            mean = jnp.sum(e * slope, axis=-1, keepdims=True) * inv
            prob = e * inv
            prob_b = prob.astype(BF)
            weight_b = (prob * ((slope - mean) * scale)).astype(BF)
            both = jnp.dot(
                prob_b, jnp.concatenate([val, vtan], axis=1), preferred_element_type=F32
            )
            tan = both[:, HD:] + jnp.dot(weight_b, val, preferred_element_type=F32)
            outs[j, 0, rows] = both[:, :HD].astype(BF).reshape(band, cols, HD)
            outs[j, 1, rows] = tan.astype(BF).reshape(band, cols, HD)

            @pl.when(me == b)
            def _():
                own_out(j).start()

            @pl.when(me != b)
            def _():
                out_copy(j, lax.rem(b - me + n, n)).start()

    for p in range(len(parts)):
        for d in range(1, n):
            for a in range(4):
                kv_copy(a, p, d).wait_send()
    for h in range(len(halos)):
        for side in range(2):
            halo_copy(side, h).wait_send()
    for j in range(hp):
        own_out(j).wait()
        for d in range(1, n):
            for a in range(2):
                q_copy(a, j, d).wait_send()
            out_copy(j, d).wait()


def shards(mesh_shape, *args):
    band, cols, width = args[0].shape
    n, n_lon = mesh_shape["lat"], mesh_shape["lon"]
    heads = width // HD
    fits = (
        heads % n == 0 and n > 1 and n_lon > 2 and n_lon % 2 == 0
        and cols == WIN and band == WIN // 2
    )
    if not fits:
        return shards_halo(*args)
    hp = heads // n
    total = band * n
    row_tab, col_tab = ray_tables(total, cols * n_lon)
    hbm = pl.BlockSpec(memory_space=pltpu.HBM)
    anywhere = pl.BlockSpec(memory_space=pl.ANY)
    q, k, v, qt, kt, vt = args
    dma = pltpu.SemaphoreType.DMA
    nq = band * cols
    nk = (band + WIN) * 2 * cols
    both = pl.pallas_call(
        functools.partial(kernel, n, n_lon, hp, band),
        out_shape=pltpu.VMEM((2, band, cols, width), BF),
        in_specs=[hbm] * 8,
        out_specs=anywhere,
        scratch_shapes=[
            pltpu.VMEM((4, total, cols, hp * HD), BF),
            pltpu.VMEM((hp, 2, total, cols, HD), BF),
            pltpu.VMEM((4, hp, total // 2, 4, cols, HD), BF),
            pltpu.VMEM((2, 4, hp, total // 2, cols, HD), BF),
            pltpu.VMEM((hp, 2, total, cols, HD), BF),
            pltpu.VMEM((2, total * cols, HD), F32),
            pltpu.VMEM((nq, nk), F32),
            pltpu.VMEM((2, total, HD), F32),
            pltpu.VMEM((2, cols, HD), F32),
            dma((4, 2, n - 1)),
            dma((4, 2, n - 1)),
            dma((hp, 2, n - 1)),
            dma((hp, 2, n - 1)),
            dma((4, 2)),
            dma((hp, 2)),
            dma((5, 2)),
            dma((5, 2)),
            dma((hp, n - 1)),
            dma((hp, n - 1)),
            dma((hp,)),
            dma((2,)),
            pltpu.SemaphoreType.REGULAR,
        ],
        compiler_params=pltpu.CompilerParams(
            collective_id=0, has_side_effects=True, vmem_limit_bytes=60 * 1024 * 1024
        ),
        name="panorama",
    )(q, k, v, qt, kt, vt, jnp.asarray(row_tab), jnp.asarray(col_tab))
    return both[0], both[1]


def solution(mesh):
    placed = (
        P("lat", "lon", None),
        P("lat", "lon", None),
        P("lat", "lon", None),
        P("lat", "lon", None),
        P("lat", "lon", None),
        P("lat", "lon", None),
    )
    return jax.shard_map(
        functools.partial(shards, dict(mesh.shape)),
        mesh=mesh,
        in_specs=placed,
        out_specs=(P("lat", "lon", None), P("lat", "lon", None)),
        check_vma=False,
    )
```

```python
import functools
import math

import jax
import jax.numpy as jnp
import numpy as np
from jax import lax
from jax.experimental import pallas as pl
from jax.experimental.pallas import tpu as pltpu
from jax.sharding import PartitionSpec as P

HD = 128
WIN = 16


def extended_2(shard, sides, width, wrap):
    for axis, dim in sides:
        count, length = (lax.axis_size(axis), shard.shape[dim])
        up = [(i, (i + 1) % count) for i in range(count if wrap else count - 1)]
        down = [(j, i) for i, j in up]
        last = lax.slice_in_dim(shard, length - width, length, axis=dim)
        leading = lax.slice_in_dim(shard, 0, width, axis=dim)
        before = lax.ppermute(last, axis, up)
        after = lax.ppermute(leading, axis, down)
        shard = jnp.concatenate([before, shard, after], axis=dim)
    return shard


def rotate_rays(values, row_first, col_first, total_rows, total_cols):
    band_rows, sector_cols, feature_width = values.shape
    quarter = HD // 4
    head_count = feature_width // HD
    frequency = (jnp.arange(quarter, dtype=jnp.int32) + 1).astype(jnp.float32)
    row_ids = (row_first + jnp.arange(band_rows, dtype=jnp.int32)).astype(jnp.float32)
    col_ids = (col_first + jnp.arange(sector_cols, dtype=jnp.int32)).astype(jnp.float32)
    lat_angle = ((row_ids + 0.5) * (math.pi / total_rows))[:, None] * frequency[None, :]
    lon_angle = (col_ids * (2.0 * math.pi / total_cols))[:, None] * frequency[None, :]
    lat_cos = jnp.cos(lat_angle)[:, None, None, :]
    lat_sin = jnp.sin(lat_angle)[:, None, None, :]
    lon_cos = jnp.cos(lon_angle)[None, :, None, :]
    lon_sin = jnp.sin(lon_angle)[None, :, None, :]
    quarters = values.astype(jnp.float32).reshape(band_rows, sector_cols, head_count, 4, quarter)
    lat_one = quarters[:, :, :, 0, :]
    lat_two = quarters[:, :, :, 1, :]
    lon_one = quarters[:, :, :, 2, :]
    lon_two = quarters[:, :, :, 3, :]
    turned = jnp.stack(
        [
            lat_one * lat_cos - lat_two * lat_sin,
            lat_one * lat_sin + lat_two * lat_cos,
            lon_one * lon_cos - lon_two * lon_sin,
            lon_one * lon_sin + lon_two * lon_cos,
        ],
        axis=3,
    )
    return turned.reshape(band_rows, sector_cols, feature_width).astype(jnp.bfloat16)


def widen_rows(stacked, radius):
    padded = extended_2(stacked, (("lat", 1),), radius, False)
    return padded[:, : padded.shape[1] - 1]


def widen_cols(stacked, radius):
    padded = extended_2(stacked, (("lon", 2),), radius, True)
    return padded[:, :, : padded.shape[2] - 1]


def shards_halo(query_tok, key_tok, value_tok, query_tan, key_tan, value_tan):
    band_rows, sector_cols, feature_width = query_tok.shape
    radius = WIN // 2
    window_span = 2 * radius
    score_scale = 1.0 / math.sqrt(HD)
    total_rows = band_rows * lax.axis_size("lat")
    total_cols = sector_cols * lax.axis_size("lon")
    row_first = lax.axis_index("lat") * band_rows
    col_first = lax.axis_index("lon") * sector_cols
    rot_query = rotate_rays(query_tok, row_first, col_first, total_rows, total_cols)
    rot_qtan = rotate_rays(query_tan, row_first, col_first, total_rows, total_cols)
    rot_key = rotate_rays(key_tok, row_first, col_first, total_rows, total_cols)
    rot_ktan = rotate_rays(key_tan, row_first, col_first, total_rows, total_cols)
    stacked = jnp.stack([rot_key, rot_ktan, value_tok, value_tan])
    extended = widen_rows(widen_cols(stacked, radius), radius)
    ext_rows = band_rows + window_span - 1
    ext_cols = sector_cols + window_span - 1
    key_count = ext_rows * ext_cols
    query_count = band_rows * sector_cols
    keys_flat = extended.reshape(4, key_count, feature_width)
    query_flat = rot_query.reshape(query_count, feature_width)
    qtan_flat = rot_qtan.reshape(query_count, feature_width)
    key_ids = jnp.arange(key_count, dtype=jnp.int32)
    query_ids = jnp.arange(query_count, dtype=jnp.int32)
    row_gap = (key_ids // ext_cols)[None, :] - (query_ids // sector_cols)[:, None]
    col_gap = (key_ids % ext_cols)[None, :] - (query_ids % sector_cols)[:, None]
    key_rows = row_first - radius + key_ids // ext_cols
    allowed = (
        (row_gap >= 0)
        & (row_gap < window_span)
        & (col_gap >= 0)
        & (col_gap < window_span)
        & ((key_rows >= 0) & (key_rows < total_rows))[None, :]
    )
    head_count = feature_width // HD
    group_size = math.gcd(head_count, 4)
    out_groups = []
    tan_groups = []
    for group_index in range(head_count // group_size):
        low_col = group_index * group_size * HD
        high_col = low_col + group_size * HD
        q_part = query_flat[:, low_col:high_col].reshape(query_count, group_size, HD)
        qt_part = qtan_flat[:, low_col:high_col].reshape(query_count, group_size, HD)
        k_part = keys_flat[0][:, low_col:high_col].reshape(key_count, group_size, HD)
        kt_part = keys_flat[1][:, low_col:high_col].reshape(key_count, group_size, HD)
        v_part = keys_flat[2][:, low_col:high_col].reshape(key_count, group_size, HD)
        vt_part = keys_flat[3][:, low_col:high_col].reshape(key_count, group_size, HD)
        scores = (
            jnp.einsum("qhd,khd->hqk", q_part, k_part, preferred_element_type=jnp.float32)
            * score_scale
        )
        scores = jnp.where(allowed[None], scores, -1e30)
        row_top = jnp.max(scores, axis=-1, keepdims=True)
        exp_scores = jnp.exp(scores - row_top)
        attention = exp_scores / jnp.sum(exp_scores, axis=-1, keepdims=True)
        slopes = (
            jnp.einsum("qhd,khd->hqk", qt_part, k_part, preferred_element_type=jnp.float32)
            + jnp.einsum("qhd,khd->hqk", q_part, kt_part, preferred_element_type=jnp.float32)
        ) * score_scale
        mean_slope = jnp.sum(attention * slopes, axis=-1, keepdims=True)
        weight_b = (attention * (slopes - mean_slope)).astype(jnp.bfloat16)
        prob_b = attention.astype(jnp.bfloat16)
        group_out = jnp.einsum("hqk,khd->qhd", prob_b, v_part, preferred_element_type=jnp.float32)
        group_tan = jnp.einsum(
            "hqk,khd->qhd", weight_b, v_part, preferred_element_type=jnp.float32
        ) + jnp.einsum("hqk,khd->qhd", prob_b, vt_part, preferred_element_type=jnp.float32)
        out_groups.append(group_out.reshape(query_count, group_size * HD))
        tan_groups.append(group_tan.reshape(query_count, group_size * HD))
    attended = jnp.concatenate(out_groups, axis=1).astype(jnp.bfloat16)
    attended_tan = jnp.concatenate(tan_groups, axis=1).astype(jnp.bfloat16)
    return (
        attended.reshape(band_rows, sector_cols, feature_width),
        attended_tan.reshape(band_rows, sector_cols, feature_width),
    )


BF = jnp.bfloat16
F32 = jnp.float32
MESH = pl.DeviceIdType.MESH


def ray_tables(total_rows, total_cols):
    quarter = HD // 4
    freq = (np.arange(quarter) + 1).astype(np.float32)
    rows = np.arange(total_rows).astype(np.float32)
    cols = np.arange(total_cols).astype(np.float32)
    lat = ((rows + np.float32(0.5)) * np.float32(math.pi / total_rows))[:, None] * freq[None, :]
    lon = (cols * np.float32(2.0 * math.pi / total_cols))[:, None] * freq[None, :]

    def table(fn, angle, first):
        part = fn(angle.astype(np.float64)).astype(np.float32)
        none = np.zeros_like(part)
        return np.concatenate([part, part, none, none] if first else [none, none, part, part], axis=1)

    row_tab = np.stack([table(np.cos, lat, True), table(np.sin, lat, True)])
    col_tab = np.stack([table(np.cos, lon, False), table(np.sin, lon, False)])
    return row_tab, col_tab


def kernel(
    n, n_lon, hp, band,
    q_ref, k_ref, v_ref, qt_ref, kt_ref, vt_ref, row_hbm, col_hbm,
    both_ref,
    raw_kv, raw_q, kvb, hs, outs, turn, bias, row_tab, col_tab,
    kv_send, kv_recv, q_send, q_recv, h_send, h_recv, o_send, o_recv, t_loc, greet,
):
    me = lax.axis_index("lat")
    lon = lax.axis_index("lon")
    left = lax.rem(lon + n_lon - 1, n_lon)
    right = lax.rem(lon + 1, n_lon)
    cols = 16
    total = n * band
    pairs = total // 2

    barrier = pltpu.get_barrier_semaphore()
    for d in range(1, n):
        pl.semaphore_signal(barrier, inc=1, device_id=(lax.rem(me + d, n), lon), device_id_type=MESH)

    def tell(sem, side):
        pl.semaphore_signal(sem, inc=1, device_id=(me, side), device_id_type=MESH)

    first, last = lon == 0, lon == n_lon - 1
    odd = lax.rem(lon, 2) == 1
    middle_odd = jnp.logical_and(odd, jnp.logical_not(last))
    middle_even = jnp.logical_and(jnp.logical_not(odd), jnp.logical_not(first))

    @pl.when(middle_odd)
    def _():
        tell(barrier, left)
        tell(barrier, right)
        pl.semaphore_wait(barrier, n - 1)

    @pl.when(middle_even)
    def _():
        pl.semaphore_wait(barrier, n + 1)
        tell(greet, left)
        tell(greet, right)

    @pl.when(first)
    def _():
        tell(barrier, left)
        pl.semaphore_wait(barrier, n)
        tell(greet, right)

    @pl.when(last)
    def _():
        tell(barrier, left)
        pl.semaphore_wait(barrier, n)
        tell(greet, right)

    kv_refs = (k_ref, kt_ref, v_ref, vt_ref)
    q_refs = (q_ref, qt_ref)
    parts = ((0, 1), (1, hp - 1)) if hp > 1 else ((0, 1),)

    def taken(ref, sem):
        pltpu.make_async_copy(ref, ref, sem).wait()

    def lanes(owner, j, count):
        return pl.ds(pl.multiple_of((owner * hp + j) * HD, HD), count * HD)

    def kv_copy(a, p, d):
        peer = lax.rem(me + d, n)
        j, count = parts[p]
        return pltpu.make_async_remote_copy(
            src_ref=kv_refs[a].at[:, :, lanes(peer, j, count)],
            dst_ref=raw_kv.at[a, pl.ds(me * band, band), :, j * HD:(j + count) * HD],
            send_sem=kv_send,
            recv_sem=kv_recv.at[p, a],
            device_id=(peer, lon),
            device_id_type=MESH,
        )

    def q_copy(a, j, d):
        peer = lax.rem(me + d, n)
        return pltpu.make_async_remote_copy(
            src_ref=q_refs[a].at[:, :, lanes(peer, j, 1)],
            dst_ref=raw_q.at[j, a, pl.ds(me * band, band)],
            send_sem=q_send,
            recv_sem=q_recv.at[j],
            device_id=(peer, lon),
            device_id_type=MESH,
        )

    def own_q(a, j):
        return pltpu.make_async_copy(
            q_refs[a].at[:, :, lanes(me, j, 1)],
            raw_q.at[j, a, pl.ds(me * band, band)],
            q_recv.at[j],
        )

    def own_copy(a, p):
        j, count = parts[p]
        return pltpu.make_async_copy(
            kv_refs[a].at[:, :, lanes(me, j, count)],
            raw_kv.at[a, pl.ds(me * band, band), :, j * HD:(j + count) * HD],
            kv_recv.at[p, a],
        )

    halos = [(0, slice(0, 4))] + [(p, slice(a, a + 1)) for p in range(1, len(parts)) for a in range(4)]

    def halo_copy(side, h):
        p, arrays = halos[h]
        j, count = parts[p]
        return pltpu.make_async_remote_copy(
            src_ref=hs.at[side, arrays, j:j + count],
            dst_ref=kvb.at[arrays, j:j + count, :, 3 - side],
            send_sem=h_send,
            recv_sem=h_recv.at[p],
            device_id=(me, right if side else left),
            device_id_type=MESH,
        )

    def out_copy(j, d):
        peer = lax.rem(me + d, n)
        return pltpu.make_async_remote_copy(
            src_ref=outs.at[j, :, pl.ds(peer * band, band)],
            dst_ref=both_ref.at[:, :, :, lanes(me, j, 1)],
            send_sem=o_send,
            recv_sem=o_recv,
            device_id=(peer, lon),
            device_id_type=MESH,
        )

    def own_out(j):
        return pltpu.make_async_copy(
            outs.at[j, :, pl.ds(me * band, band)],
            both_ref.at[:, :, :, lanes(me, j, 1)],
            o_recv,
        )

    here = pl.ds(pl.multiple_of(lon * cols, cols), cols)
    row_copy = pltpu.make_async_copy(row_hbm, row_tab, t_loc.at[0])
    col_copy = pltpu.make_async_copy(col_hbm.at[:, here], col_tab, t_loc.at[1])
    row_copy.start()
    col_copy.start()
    for p in range(len(parts)):
        for a in range(4):
            for d in range(1, n):
                kv_copy(a, p, d).start()
        for a in range(4):
            own_copy(a, p).start()
    for j in range(hp):
        for a in range(2):
            for d in range(1, n):
                q_copy(a, j, d).start()
        for a in range(2):
            own_q(a, j).start()

    row_copy.wait()
    col_copy.wait()
    for t in range(2):
        whole = row_tab[t][:, None, :] + col_tab[t][None, :, :]
        turn[t] = whole.reshape(total * cols, HD)
    shape = (band * cols, (band + WIN) * 2 * cols)
    query = lax.broadcasted_iota(jnp.int32, shape, 0)
    key = lax.broadcasted_iota(jnp.int32, shape, 1)
    part = (key % 64) // 16
    spot = key % 16
    own = part < 2
    key_row = (key // 64) * 2 + jnp.where(own, part, spot // 8)
    key_col = jnp.where(own, spot, jnp.where(part == 2, spot % 8 - 8, spot % 8 + 16))
    row_gap = key_row - query // 16
    col_gap = key_col - query % 16 + WIN // 2
    allowed = (row_gap >= 0) & (row_gap < WIN) & (col_gap >= 0) & (col_gap < WIN)
    bias[...] = jnp.where(allowed, 0.0, -1e30)
    src = lax.broadcasted_iota(jnp.int32, (HD, HD), 0)
    dst = lax.broadcasted_iota(jnp.int32, (HD, HD), 1)
    low = (dst % 64) < 32
    swap = (
        jnp.where(low & (src == dst + 32), -1.0, 0.0)
        + jnp.where(jnp.logical_not(low) & (src == dst - 32), 1.0, 0.0)
    ).astype(BF)

    def turned(x):
        flat = x.reshape(total * cols, HD)
        other = jnp.dot(flat, swap, preferred_element_type=F32)
        return flat.astype(F32) * turn[0] + other * turn[1]

    def stage(a, j):
        x = raw_kv[a, :, :, pl.ds(pl.multiple_of(j * HD, HD), HD)]
        y = turned(x) if a < 2 else x.reshape(total * cols, HD).astype(F32)
        kvb[a, j, :, 0:2] = y.reshape(pairs, 2, cols, HD).astype(BF)
        halves = y.reshape(total, 2, cols // 2, HD)
        for side in range(2):
            hs[side, a, j] = halves[:, side].reshape(pairs, cols, HD).astype(BF)

    @pl.when(middle_odd)
    def _():
        pl.semaphore_wait(greet, 2)

    @pl.when(jnp.logical_or(first, last))
    def _():
        pl.semaphore_wait(greet, 1)

    for p in range(len(parts)):
        for a in range(4):
            j, count = parts[p]
            taken(raw_kv.at[a, :, :, j * HD:(j + count) * HD], kv_recv.at[p, a])
            if parts[p][1] == 1:
                stage(a, parts[p][0])
            else:
                pl.loop(parts[p][0], sum(parts[p]))(functools.partial(stage, a))
            for h in range(len(halos)):
                if halos[h][0] == p and halos[h][1].stop == a + 1:
                    for side in range(2):
                        halo_copy(side, h).start()

    scale2 = math.log2(math.e) / math.sqrt(HD)
    scale = 1.0 / math.sqrt(HD)

    @pl.loop(0, hp)
    def _(j):
        for p in range(len(parts)):
            @pl.when(j == parts[p][0])
            def _():
                taken(kvb.at[:, parts[p][0]:sum(parts[p]), :, 2:4], h_recv.at[p])

        taken(raw_q.at[j], q_recv.at[j])
        for a in range(2):
            raw_q[j, a] = turned(raw_q[j, a]).astype(BF).reshape(total, cols, HD)
        nq = band * cols
        for b in range(n):
            first = max(0, b * band - WIN // 2)
            last = min(total, (b + 1) * band + WIN // 2)
            skip = (first - (b * band - WIN // 2)) // 2 * 64
            p0, p1 = first // 2, last // 2
            nk = (p1 - p0) * 64
            keys = kvb[0, j, p0:p1].reshape(nk, HD)
            ktan = kvb[1, j, p0:p1].reshape(nk, HD)
            val = kvb[2, j, p0:p1].reshape(nk, HD)
            vtan = kvb[3, j, p0:p1].reshape(nk, HD)
            rows = slice(b * band, (b + 1) * band)
            q = raw_q[j, 0, rows].reshape(nq, HD)
            qt = raw_q[j, 1, rows].reshape(nq, HD)
            nt = (((1,), (1,)), ((), ()))
            score = lax.dot_general(q, keys, nt, preferred_element_type=F32)
            score = score * scale2 + bias[:, skip:skip + nk]
            top = jnp.max(score, axis=-1, keepdims=True)
            e = jnp.exp2(score - top)
            inv = 1.0 / jnp.sum(e, axis=-1, keepdims=True)
            slope = lax.dot_general(
                jnp.concatenate([qt, q], axis=1),
                jnp.concatenate([keys, ktan], axis=1),
                nt,
                preferred_element_type=F32,
            )
            mean = jnp.sum(e * slope, axis=-1, keepdims=True) * inv
            prob = e * inv
            prob_b = prob.astype(BF)
            weight_b = (prob * ((slope - mean) * scale)).astype(BF)
            both = jnp.dot(
                prob_b, jnp.concatenate([val, vtan], axis=1), preferred_element_type=F32
            )
            tan = both[:, HD:] + jnp.dot(weight_b, val, preferred_element_type=F32)
            outs[j, 0, rows] = both[:, :HD].astype(BF).reshape(band, cols, HD)
            outs[j, 1, rows] = tan.astype(BF).reshape(band, cols, HD)

            @pl.when(me == b)
            def _():
                own_out(j).start()

            @pl.when(me != b)
            def _():
                out_copy(j, lax.rem(b - me + n, n)).start()

    taken(raw_kv.at[:, 0:total - band], kv_send)
    taken(raw_q.at[:, :, 0:total - band], q_send)
    taken(hs, h_send)
    taken(outs.at[:, :, 0:total - band], o_send)
    taken(both_ref, o_recv)


def shards(mesh_shape, *args):
    band, cols, width = args[0].shape
    n, n_lon = mesh_shape["lat"], mesh_shape["lon"]
    heads = width // HD
    fits = (
        heads % n == 0 and n > 1 and n_lon > 2 and n_lon % 2 == 0
        and cols == WIN and band == WIN // 2
    )
    if not fits:
        return shards_halo(*args)
    hp = heads // n
    total = band * n
    row_tab, col_tab = ray_tables(total, cols * n_lon)
    hbm = pl.BlockSpec(memory_space=pltpu.HBM)
    anywhere = pl.BlockSpec(memory_space=pl.ANY)
    q, k, v, qt, kt, vt = args
    dma = pltpu.SemaphoreType.DMA
    nq = band * cols
    nk = (band + WIN) * 2 * cols
    both = pl.pallas_call(
        functools.partial(kernel, n, n_lon, hp, band),
        out_shape=pltpu.VMEM((2, band, cols, width), BF),
        in_specs=[hbm] * 8,
        out_specs=anywhere,
        scratch_shapes=[
            pltpu.VMEM((4, total, cols, hp * HD), BF),
            pltpu.VMEM((hp, 2, total, cols, HD), BF),
            pltpu.VMEM((4, hp, total // 2, 4, cols, HD), BF),
            pltpu.VMEM((2, 4, hp, total // 2, cols, HD), BF),
            pltpu.VMEM((hp, 2, total, cols, HD), BF),
            pltpu.VMEM((2, total * cols, HD), F32),
            pltpu.VMEM((nq, nk), F32),
            pltpu.VMEM((2, total, HD), F32),
            pltpu.VMEM((2, cols, HD), F32),
            dma,
            dma((2, 4)),
            dma,
            dma((hp,)),
            dma,
            dma((2,)),
            dma,
            dma,
            dma((2,)),
            pltpu.SemaphoreType.REGULAR,
        ],
        compiler_params=pltpu.CompilerParams(
            collective_id=0, has_side_effects=True, vmem_limit_bytes=60 * 1024 * 1024
        ),
        name="panorama",
    )(q, k, v, qt, kt, vt, jnp.asarray(row_tab), jnp.asarray(col_tab))
    return both[0], both[1]


def solution(mesh):
    placed = (
        P("lat", "lon", None),
        P("lat", "lon", None),
        P("lat", "lon", None),
        P("lat", "lon", None),
        P("lat", "lon", None),
        P("lat", "lon", None),
    )
    return jax.shard_map(
        functools.partial(shards, dict(mesh.shape)),
        mesh=mesh,
        in_specs=placed,
        out_specs=(P("lat", "lon", None), P("lat", "lon", None)),
        check_vma=False,
    )
```

```python
import functools
import math

import jax
import jax.numpy as jnp
import numpy as np
from jax import lax
from jax.experimental import pallas as pl
from jax.experimental.pallas import tpu as pltpu
from jax.sharding import PartitionSpec as P

HD = 128
WIN = 16


def extended_2(shard, sides, width, wrap):
    for axis, dim in sides:
        count, length = (lax.axis_size(axis), shard.shape[dim])
        up = [(i, (i + 1) % count) for i in range(count if wrap else count - 1)]
        down = [(j, i) for i, j in up]
        last = lax.slice_in_dim(shard, length - width, length, axis=dim)
        leading = lax.slice_in_dim(shard, 0, width, axis=dim)
        before = lax.ppermute(last, axis, up)
        after = lax.ppermute(leading, axis, down)
        shard = jnp.concatenate([before, shard, after], axis=dim)
    return shard


def rotate_rays(values, row_first, col_first, total_rows, total_cols):
    band_rows, sector_cols, feature_width = values.shape
    quarter = HD // 4
    head_count = feature_width // HD
    frequency = (jnp.arange(quarter, dtype=jnp.int32) + 1).astype(jnp.float32)
    row_ids = (row_first + jnp.arange(band_rows, dtype=jnp.int32)).astype(jnp.float32)
    col_ids = (col_first + jnp.arange(sector_cols, dtype=jnp.int32)).astype(jnp.float32)
    lat_angle = ((row_ids + 0.5) * (math.pi / total_rows))[:, None] * frequency[None, :]
    lon_angle = (col_ids * (2.0 * math.pi / total_cols))[:, None] * frequency[None, :]
    lat_cos = jnp.cos(lat_angle)[:, None, None, :]
    lat_sin = jnp.sin(lat_angle)[:, None, None, :]
    lon_cos = jnp.cos(lon_angle)[None, :, None, :]
    lon_sin = jnp.sin(lon_angle)[None, :, None, :]
    quarters = values.astype(jnp.float32).reshape(band_rows, sector_cols, head_count, 4, quarter)
    lat_one = quarters[:, :, :, 0, :]
    lat_two = quarters[:, :, :, 1, :]
    lon_one = quarters[:, :, :, 2, :]
    lon_two = quarters[:, :, :, 3, :]
    turned = jnp.stack(
        [
            lat_one * lat_cos - lat_two * lat_sin,
            lat_one * lat_sin + lat_two * lat_cos,
            lon_one * lon_cos - lon_two * lon_sin,
            lon_one * lon_sin + lon_two * lon_cos,
        ],
        axis=3,
    )
    return turned.reshape(band_rows, sector_cols, feature_width).astype(jnp.bfloat16)


def widen_rows(stacked, radius):
    padded = extended_2(stacked, (("lat", 1),), radius, False)
    return padded[:, : padded.shape[1] - 1]


def widen_cols(stacked, radius):
    padded = extended_2(stacked, (("lon", 2),), radius, True)
    return padded[:, :, : padded.shape[2] - 1]


def shards_halo(query_tok, key_tok, value_tok, query_tan, key_tan, value_tan):
    band_rows, sector_cols, feature_width = query_tok.shape
    radius = WIN // 2
    window_span = 2 * radius
    score_scale = 1.0 / math.sqrt(HD)
    total_rows = band_rows * lax.axis_size("lat")
    total_cols = sector_cols * lax.axis_size("lon")
    row_first = lax.axis_index("lat") * band_rows
    col_first = lax.axis_index("lon") * sector_cols
    rot_query = rotate_rays(query_tok, row_first, col_first, total_rows, total_cols)
    rot_qtan = rotate_rays(query_tan, row_first, col_first, total_rows, total_cols)
    rot_key = rotate_rays(key_tok, row_first, col_first, total_rows, total_cols)
    rot_ktan = rotate_rays(key_tan, row_first, col_first, total_rows, total_cols)
    stacked = jnp.stack([rot_key, rot_ktan, value_tok, value_tan])
    extended = widen_rows(widen_cols(stacked, radius), radius)
    ext_rows = band_rows + window_span - 1
    ext_cols = sector_cols + window_span - 1
    key_count = ext_rows * ext_cols
    query_count = band_rows * sector_cols
    keys_flat = extended.reshape(4, key_count, feature_width)
    query_flat = rot_query.reshape(query_count, feature_width)
    qtan_flat = rot_qtan.reshape(query_count, feature_width)
    key_ids = jnp.arange(key_count, dtype=jnp.int32)
    query_ids = jnp.arange(query_count, dtype=jnp.int32)
    row_gap = (key_ids // ext_cols)[None, :] - (query_ids // sector_cols)[:, None]
    col_gap = (key_ids % ext_cols)[None, :] - (query_ids % sector_cols)[:, None]
    key_rows = row_first - radius + key_ids // ext_cols
    allowed = (
        (row_gap >= 0)
        & (row_gap < window_span)
        & (col_gap >= 0)
        & (col_gap < window_span)
        & ((key_rows >= 0) & (key_rows < total_rows))[None, :]
    )
    head_count = feature_width // HD
    group_size = math.gcd(head_count, 4)
    out_groups = []
    tan_groups = []
    for group_index in range(head_count // group_size):
        low_col = group_index * group_size * HD
        high_col = low_col + group_size * HD
        q_part = query_flat[:, low_col:high_col].reshape(query_count, group_size, HD)
        qt_part = qtan_flat[:, low_col:high_col].reshape(query_count, group_size, HD)
        k_part = keys_flat[0][:, low_col:high_col].reshape(key_count, group_size, HD)
        kt_part = keys_flat[1][:, low_col:high_col].reshape(key_count, group_size, HD)
        v_part = keys_flat[2][:, low_col:high_col].reshape(key_count, group_size, HD)
        vt_part = keys_flat[3][:, low_col:high_col].reshape(key_count, group_size, HD)
        scores = (
            jnp.einsum("qhd,khd->hqk", q_part, k_part, preferred_element_type=jnp.float32)
            * score_scale
        )
        scores = jnp.where(allowed[None], scores, -1e30)
        row_top = jnp.max(scores, axis=-1, keepdims=True)
        exp_scores = jnp.exp(scores - row_top)
        attention = exp_scores / jnp.sum(exp_scores, axis=-1, keepdims=True)
        slopes = (
            jnp.einsum("qhd,khd->hqk", qt_part, k_part, preferred_element_type=jnp.float32)
            + jnp.einsum("qhd,khd->hqk", q_part, kt_part, preferred_element_type=jnp.float32)
        ) * score_scale
        mean_slope = jnp.sum(attention * slopes, axis=-1, keepdims=True)
        weight_b = (attention * (slopes - mean_slope)).astype(jnp.bfloat16)
        prob_b = attention.astype(jnp.bfloat16)
        group_out = jnp.einsum("hqk,khd->qhd", prob_b, v_part, preferred_element_type=jnp.float32)
        group_tan = jnp.einsum(
            "hqk,khd->qhd", weight_b, v_part, preferred_element_type=jnp.float32
        ) + jnp.einsum("hqk,khd->qhd", prob_b, vt_part, preferred_element_type=jnp.float32)
        out_groups.append(group_out.reshape(query_count, group_size * HD))
        tan_groups.append(group_tan.reshape(query_count, group_size * HD))
    attended = jnp.concatenate(out_groups, axis=1).astype(jnp.bfloat16)
    attended_tan = jnp.concatenate(tan_groups, axis=1).astype(jnp.bfloat16)
    return (
        attended.reshape(band_rows, sector_cols, feature_width),
        attended_tan.reshape(band_rows, sector_cols, feature_width),
    )


BF = jnp.bfloat16
F32 = jnp.float32
MESH = pl.DeviceIdType.MESH


def ray_tables(total_rows, total_cols):
    quarter = HD // 4
    freq = (np.arange(quarter) + 1).astype(np.float32)
    rows = np.arange(total_rows).astype(np.float32)
    cols = np.arange(total_cols).astype(np.float32)
    lat = ((rows + np.float32(0.5)) * np.float32(math.pi / total_rows))[:, None] * freq[None, :]
    lon = (cols * np.float32(2.0 * math.pi / total_cols))[:, None] * freq[None, :]

    def table(fn, angle, first):
        part = fn(angle.astype(np.float64)).astype(np.float32)
        none = np.zeros_like(part)
        return np.concatenate([part, part, none, none] if first else [none, none, part, part], axis=1)

    row_tab = np.stack([table(np.cos, lat, True), table(np.sin, lat, True)])
    col_tab = np.stack([table(np.cos, lon, False), table(np.sin, lon, False)])
    return row_tab, col_tab


def kernel(
    n, n_lon, hp, band,
    q_ref, k_ref, v_ref, qt_ref, kt_ref, vt_ref, row_hbm, col_hbm,
    both_ref,
    raw_kv, raw_q, kvb, hs, outs, turn, bias, row_tab, col_tab,
    kv_send, kv_recv, q_send, q_recv, h_send, h_recv, o_send, o_recv, t_loc, greet, near, peers,
):
    me = lax.axis_index("lat")
    lon = lax.axis_index("lon")
    left = lax.rem(lon + n_lon - 1, n_lon)
    right = lax.rem(lon + 1, n_lon)
    cols = 16
    total = n * band
    pairs = total // 2

    def told(sem, lat, sector):
        pl.semaphore_signal(sem, inc=1, device_id=(lat, sector), device_id_type=MESH)

    barrier = pltpu.get_barrier_semaphore()
    lead, late = me == 0, me == n - 1
    middle = jnp.logical_not(jnp.logical_or(lead, late))
    first, last = lon == 0, lon == n_lon - 1
    odd = lax.rem(lon, 2) == 1
    middle_odd = jnp.logical_and(odd, jnp.logical_not(last))
    middle_even = jnp.logical_and(jnp.logical_not(odd), jnp.logical_not(first))

    @pl.when(lead)
    def _():
        for d in range(1, n):
            told(barrier, d, lon)

    @pl.when(middle)
    def _():
        told(barrier, 0, lon)
        told(barrier, n - 1, lon)

    @pl.when(jnp.logical_and(lead, jnp.logical_or(odd, first)))
    def _():
        told(barrier, me, left)

    @pl.when(jnp.logical_and(lead, middle_odd))
    def _():
        told(barrier, me, right)

    kv_refs = (k_ref, kt_ref, v_ref, vt_ref)
    q_refs = (q_ref, qt_ref)
    parts = tuple((j, 1) for j in range(hp))
    order = (0, *range(n - 2, 0, -1), n - 1)

    def taken(ref, sem):
        pltpu.make_async_copy(ref, ref, sem).wait()

    def lanes(owner, j, count):
        return pl.ds(pl.multiple_of((owner * hp + j) * HD, HD), count * HD)

    def kv_copy(a, p, peer):
        j, count = parts[p]
        return pltpu.make_async_remote_copy(
            src_ref=kv_refs[a].at[:, :, lanes(peer, j, count)],
            dst_ref=raw_kv.at[a, pl.ds(me * band, band), :, j * HD:(j + count) * HD],
            send_sem=kv_send,
            recv_sem=kv_recv.at[p, a],
            device_id=(peer, lon),
            device_id_type=MESH,
        )

    def q_copy(a, j, peer):
        return pltpu.make_async_remote_copy(
            src_ref=q_refs[a].at[:, :, lanes(peer, j, 1)],
            dst_ref=raw_q.at[j, a, pl.ds(me * band, band)],
            send_sem=q_send,
            recv_sem=q_recv.at[j],
            device_id=(peer, lon),
            device_id_type=MESH,
        )

    def own_q(a, j):
        return pltpu.make_async_copy(
            q_refs[a].at[:, :, lanes(me, j, 1)],
            raw_q.at[j, a, pl.ds(me * band, band)],
            q_recv.at[j],
        )

    def own_copy(a, p):
        j, count = parts[p]
        return pltpu.make_async_copy(
            kv_refs[a].at[:, :, lanes(me, j, count)],
            raw_kv.at[a, pl.ds(me * band, band), :, j * HD:(j + count) * HD],
            kv_recv.at[p, a],
        )

    halos = [(p, slice(0, 4)) for p in range(hp - 1)] + [(hp - 1, slice(a, a + 1)) for a in range(4)]

    def halo_copy(side, h):
        p, arrays = halos[h]
        j, count = parts[p]
        return pltpu.make_async_remote_copy(
            src_ref=hs.at[side, arrays, j:j + count],
            dst_ref=kvb.at[arrays, j:j + count, :, 3 - side],
            send_sem=h_send,
            recv_sem=h_recv.at[p],
            device_id=(me, right if side else left),
            device_id_type=MESH,
        )

    def out_copy(j, d):
        peer = lax.rem(me + d, n)
        return pltpu.make_async_remote_copy(
            src_ref=outs.at[j, :, pl.ds(peer * band, band)],
            dst_ref=both_ref.at[:, :, :, lanes(me, j, 1)],
            send_sem=o_send,
            recv_sem=o_recv,
            device_id=(peer, lon),
            device_id_type=MESH,
        )

    def own_out(j):
        return pltpu.make_async_copy(
            outs.at[j, :, pl.ds(me * band, band)],
            both_ref.at[:, :, :, lanes(me, j, 1)],
            o_recv,
        )

    here = pl.ds(pl.multiple_of(lon * cols, cols), cols)
    row_copy = pltpu.make_async_copy(row_hbm, row_tab, t_loc.at[0])
    col_copy = pltpu.make_async_copy(col_hbm.at[:, here], col_tab, t_loc.at[1])
    row_copy.start()
    col_copy.start()

    @pl.when(late)
    def _():
        pl.semaphore_wait(barrier, n - 1)
        for d in range(n - 1):
            told(peers, d, lon)

    @pl.when(middle)
    def _():
        pl.semaphore_wait(barrier, 1)

    @pl.when(jnp.logical_and(lead, middle_odd))
    def _():
        pl.semaphore_wait(barrier, n - 2)

    @pl.when(jnp.logical_and(lead, middle_even))
    def _():
        pl.semaphore_wait(barrier, n)

    @pl.when(jnp.logical_and(lead, jnp.logical_or(first, last)))
    def _():
        pl.semaphore_wait(barrier, n - 1)

    @pl.when(jnp.logical_not(lead))
    def _():
        for a in range(4):
            kv_copy(a, 0, 0).start()

    @pl.when(lead)
    def _():
        for d in range(1, n - 1):
            for a in range(4):
                kv_copy(a, 0, d).start()

    @pl.when(jnp.logical_not(late))
    def _():
        pl.semaphore_wait(peers, 1)

    @pl.when(jnp.logical_and(lead, middle_even))
    def _():
        told(near.at[1], me, left)
        told(near.at[0], me, right)

    @pl.when(jnp.logical_and(lead, jnp.logical_or(first, last)))
    def _():
        told(near.at[0], me, right)

    @pl.when(lead)
    def _():
        for a in range(4):
            kv_copy(a, 0, n - 1).start()

    for peer in order[1:]:
        @pl.when(jnp.logical_not(jnp.logical_or(lead, peer == me)))
        def _():
            for a in range(4):
                kv_copy(a, 0, peer).start()

    for a in range(4):
        own_copy(a, 0).start()
    for p in range(1, len(parts)):
        for peer in order:
            @pl.when(peer != me)
            def _():
                for a in range(4):
                    kv_copy(a, p, peer).start()

        for a in range(4):
            own_copy(a, p).start()
    for j in range(hp):
        for peer in order:
            @pl.when(peer != me)
            def _():
                for a in range(2):
                    q_copy(a, j, peer).start()

        for a in range(2):
            own_q(a, j).start()

    row_copy.wait()
    col_copy.wait()
    for t in range(2):
        whole = row_tab[t][:, None, :] + col_tab[t][None, :, :]
        turn[t] = whole.reshape(total * cols, HD)
    shape = (band * cols, (band + WIN) * 2 * cols)
    query = lax.broadcasted_iota(jnp.int32, shape, 0)
    key = lax.broadcasted_iota(jnp.int32, shape, 1)
    part = (key % 64) // 16
    spot = key % 16
    own = part < 2
    key_row = (key // 64) * 2 + jnp.where(own, part, spot // 8)
    key_col = jnp.where(own, spot, jnp.where(part == 2, spot % 8 - 8, spot % 8 + 16))
    row_gap = key_row - query // 16
    col_gap = key_col - query % 16 + WIN // 2
    allowed = (row_gap >= 0) & (row_gap < WIN) & (col_gap >= 0) & (col_gap < WIN)
    bias[...] = jnp.where(allowed, 0.0, -1e30)
    src = lax.broadcasted_iota(jnp.int32, (HD, HD), 0)
    dst = lax.broadcasted_iota(jnp.int32, (HD, HD), 1)
    low = (dst % 64) < 32
    swap = (
        jnp.where(low & (src == dst + 32), -1.0, 0.0)
        + jnp.where(jnp.logical_not(low) & (src == dst - 32), 1.0, 0.0)
    ).astype(BF)

    def turned(x):
        flat = x.reshape(total * cols, HD)
        other = jnp.dot(flat, swap, preferred_element_type=F32)
        return flat.astype(F32) * turn[0] + other * turn[1]

    def stage(a, j):
        x = raw_kv[a, :, :, pl.ds(pl.multiple_of(j * HD, HD), HD)]
        y = turned(x) if a < 2 else x.reshape(total * cols, HD).astype(F32)
        kvb[a, j, :, 0:2] = y.reshape(pairs, 2, cols, HD).astype(BF)
        halves = y.reshape(total, 2, cols // 2, HD)
        for side in range(2):
            hs[side, a, j] = halves[:, side].reshape(pairs, cols, HD).astype(BF)

    @pl.when(lead)
    def _():
        pl.semaphore_wait(near.at[0], 1)

        @pl.when(jnp.logical_or(middle_odd, last))
        def _():
            told(near.at[1], me, left)

        pl.semaphore_wait(near.at[1], 1)

        @pl.when(middle_odd)
        def _():
            told(near.at[0], me, right)

        @pl.when(first)
        def _():
            told(near.at[1], me, left)

        for d in range(1, n):
            told(greet, lax.rem(me + d, n), lon)

    for p in range(len(parts)):
        for a in range(4):
            j, count = parts[p]
            taken(raw_kv.at[a, :, :, j * HD:(j + count) * HD], kv_recv.at[p, a])
            if parts[p][1] == 1:
                stage(a, parts[p][0])
            else:
                pl.loop(parts[p][0], sum(parts[p]))(functools.partial(stage, a))
            if p == 0 and a == 0:
                @pl.when(jnp.logical_not(lead))
                def _():
                    pl.semaphore_wait(greet, 1)

            for h in range(len(halos)):
                if halos[h][0] == p and halos[h][1].stop == a + 1:
                    for side in range(2):
                        halo_copy(side, h).start()

    scale2 = math.log2(math.e) / math.sqrt(HD)
    scale = 1.0 / math.sqrt(HD)

    @pl.loop(0, hp)
    def _(j):
        for p in range(len(parts)):
            @pl.when(j == parts[p][0])
            def _():
                taken(kvb.at[:, parts[p][0]:sum(parts[p]), :, 2:4], h_recv.at[p])

        taken(raw_q.at[j], q_recv.at[j])
        for a in range(2):
            raw_q[j, a] = turned(raw_q[j, a]).astype(BF).reshape(total, cols, HD)
        nq = band * cols
        for b in order:
            first = max(0, b * band - WIN // 2)
            last = min(total, (b + 1) * band + WIN // 2)
            skip = (first - (b * band - WIN // 2)) // 2 * 64
            p0, p1 = first // 2, last // 2
            nk = (p1 - p0) * 64
            keys = kvb[0, j, p0:p1].reshape(nk, HD)
            ktan = kvb[1, j, p0:p1].reshape(nk, HD)
            val = kvb[2, j, p0:p1].reshape(nk, HD)
            vtan = kvb[3, j, p0:p1].reshape(nk, HD)
            rows = slice(b * band, (b + 1) * band)
            q = raw_q[j, 0, rows].reshape(nq, HD)
            qt = raw_q[j, 1, rows].reshape(nq, HD)
            nt = (((1,), (1,)), ((), ()))
            score = lax.dot_general(q, keys, nt, preferred_element_type=F32)
            score = score * scale2 + bias[:, skip:skip + nk]
            top = jnp.max(score, axis=-1, keepdims=True)
            e = jnp.exp2(score - top)
            inv = 1.0 / jnp.sum(e, axis=-1, keepdims=True)
            slope = lax.dot_general(
                jnp.concatenate([qt, q], axis=1),
                jnp.concatenate([keys, ktan], axis=1),
                nt,
                preferred_element_type=F32,
            )
            mean = jnp.sum(e * slope, axis=-1, keepdims=True) * inv
            prob = e * inv
            prob_b = prob.astype(BF)
            weight_b = (prob * ((slope - mean) * scale)).astype(BF)
            both = jnp.dot(
                prob_b, jnp.concatenate([val, vtan], axis=1), preferred_element_type=F32
            )
            tan = both[:, HD:] + jnp.dot(weight_b, val, preferred_element_type=F32)
            outs[j, 0, rows] = both[:, :HD].astype(BF).reshape(band, cols, HD)
            outs[j, 1, rows] = tan.astype(BF).reshape(band, cols, HD)

            @pl.when(me == b)
            def _():
                own_out(j).start()

            @pl.when(me != b)
            def _():
                out_copy(j, lax.rem(b - me + n, n)).start()

    taken(raw_kv.at[:, 0:total - band], kv_send)
    taken(raw_q.at[:, :, 0:total - band], q_send)
    taken(hs, h_send)
    taken(outs.at[:, :, 0:total - band], o_send)
    taken(both_ref, o_recv)


def shards(mesh_shape, *args):
    band, cols, width = args[0].shape
    n, n_lon = mesh_shape["lat"], mesh_shape["lon"]
    heads = width // HD
    fits = (
        heads % n == 0 and n > 1 and n_lon > 2 and n_lon % 2 == 0
        and cols == WIN and band == WIN // 2
    )
    if not fits:
        return shards_halo(*args)
    hp = heads // n
    total = band * n
    row_tab, col_tab = ray_tables(total, cols * n_lon)
    hbm = pl.BlockSpec(memory_space=pltpu.HBM)
    anywhere = pl.BlockSpec(memory_space=pl.ANY)
    q, k, v, qt, kt, vt = args
    dma = pltpu.SemaphoreType.DMA
    nq = band * cols
    nk = (band + WIN) * 2 * cols
    both = pl.pallas_call(
        functools.partial(kernel, n, n_lon, hp, band),
        out_shape=pltpu.VMEM((2, band, cols, width), BF),
        in_specs=[hbm] * 8,
        out_specs=anywhere,
        scratch_shapes=[
            pltpu.VMEM((4, total, cols, hp * HD), BF),
            pltpu.VMEM((hp, 2, total, cols, HD), BF),
            pltpu.VMEM((4, hp, total // 2, 4, cols, HD), BF),
            pltpu.VMEM((2, 4, hp, total // 2, cols, HD), BF),
            pltpu.VMEM((hp, 2, total, cols, HD), BF),
            pltpu.VMEM((2, total * cols, HD), F32),
            pltpu.VMEM((nq, nk), F32),
            pltpu.VMEM((2, total, HD), F32),
            pltpu.VMEM((2, cols, HD), F32),
            dma,
            dma((hp, 4)),
            dma,
            dma((hp,)),
            dma,
            dma((hp,)),
            dma,
            dma,
            dma((2,)),
            pltpu.SemaphoreType.REGULAR,
            pltpu.SemaphoreType.REGULAR((2,)),
            pltpu.SemaphoreType.REGULAR,
        ],
        compiler_params=pltpu.CompilerParams(
            collective_id=0, has_side_effects=True, vmem_limit_bytes=60 * 1024 * 1024
        ),
        name="panorama",
    )(q, k, v, qt, kt, vt, jnp.asarray(row_tab), jnp.asarray(col_tab))
    return both[0], both[1]


def solution(mesh):
    placed = (
        P("lat", "lon", None),
        P("lat", "lon", None),
        P("lat", "lon", None),
        P("lat", "lon", None),
        P("lat", "lon", None),
        P("lat", "lon", None),
    )
    return jax.shard_map(
        functools.partial(shards, dict(mesh.shape)),
        mesh=mesh,
        in_specs=placed,
        out_specs=(P("lat", "lon", None), P("lat", "lon", None)),
        check_vma=False,
    )
```

```python
import functools
import math

import jax
import jax.numpy as jnp
import numpy as np
from jax import lax
from jax.experimental import pallas as pl
from jax.experimental.pallas import tpu as pltpu
from jax.sharding import PartitionSpec as P

HD = 128
WIN = 16


def extended_2(shard, sides, width, wrap):
    for axis, dim in sides:
        count, length = (lax.axis_size(axis), shard.shape[dim])
        up = [(i, (i + 1) % count) for i in range(count if wrap else count - 1)]
        down = [(j, i) for i, j in up]
        last = lax.slice_in_dim(shard, length - width, length, axis=dim)
        leading = lax.slice_in_dim(shard, 0, width, axis=dim)
        before = lax.ppermute(last, axis, up)
        after = lax.ppermute(leading, axis, down)
        shard = jnp.concatenate([before, shard, after], axis=dim)
    return shard


def rotate_rays(values, row_first, col_first, total_rows, total_cols):
    band_rows, sector_cols, feature_width = values.shape
    quarter = HD // 4
    head_count = feature_width // HD
    frequency = (jnp.arange(quarter, dtype=jnp.int32) + 1).astype(jnp.float32)
    row_ids = (row_first + jnp.arange(band_rows, dtype=jnp.int32)).astype(jnp.float32)
    col_ids = (col_first + jnp.arange(sector_cols, dtype=jnp.int32)).astype(jnp.float32)
    lat_angle = ((row_ids + 0.5) * (math.pi / total_rows))[:, None] * frequency[None, :]
    lon_angle = (col_ids * (2.0 * math.pi / total_cols))[:, None] * frequency[None, :]
    lat_cos = jnp.cos(lat_angle)[:, None, None, :]
    lat_sin = jnp.sin(lat_angle)[:, None, None, :]
    lon_cos = jnp.cos(lon_angle)[None, :, None, :]
    lon_sin = jnp.sin(lon_angle)[None, :, None, :]
    quarters = values.astype(jnp.float32).reshape(band_rows, sector_cols, head_count, 4, quarter)
    lat_one = quarters[:, :, :, 0, :]
    lat_two = quarters[:, :, :, 1, :]
    lon_one = quarters[:, :, :, 2, :]
    lon_two = quarters[:, :, :, 3, :]
    turned = jnp.stack(
        [
            lat_one * lat_cos - lat_two * lat_sin,
            lat_one * lat_sin + lat_two * lat_cos,
            lon_one * lon_cos - lon_two * lon_sin,
            lon_one * lon_sin + lon_two * lon_cos,
        ],
        axis=3,
    )
    return turned.reshape(band_rows, sector_cols, feature_width).astype(jnp.bfloat16)


def widen_rows(stacked, radius):
    padded = extended_2(stacked, (("lat", 1),), radius, False)
    return padded[:, : padded.shape[1] - 1]


def widen_cols(stacked, radius):
    padded = extended_2(stacked, (("lon", 2),), radius, True)
    return padded[:, :, : padded.shape[2] - 1]


def shards_halo(query_tok, key_tok, value_tok, query_tan, key_tan, value_tan):
    band_rows, sector_cols, feature_width = query_tok.shape
    radius = WIN // 2
    window_span = 2 * radius
    score_scale = 1.0 / math.sqrt(HD)
    total_rows = band_rows * lax.axis_size("lat")
    total_cols = sector_cols * lax.axis_size("lon")
    row_first = lax.axis_index("lat") * band_rows
    col_first = lax.axis_index("lon") * sector_cols
    rot_query = rotate_rays(query_tok, row_first, col_first, total_rows, total_cols)
    rot_qtan = rotate_rays(query_tan, row_first, col_first, total_rows, total_cols)
    rot_key = rotate_rays(key_tok, row_first, col_first, total_rows, total_cols)
    rot_ktan = rotate_rays(key_tan, row_first, col_first, total_rows, total_cols)
    stacked = jnp.stack([rot_key, rot_ktan, value_tok, value_tan])
    extended = widen_rows(widen_cols(stacked, radius), radius)
    ext_rows = band_rows + window_span - 1
    ext_cols = sector_cols + window_span - 1
    key_count = ext_rows * ext_cols
    query_count = band_rows * sector_cols
    keys_flat = extended.reshape(4, key_count, feature_width)
    query_flat = rot_query.reshape(query_count, feature_width)
    qtan_flat = rot_qtan.reshape(query_count, feature_width)
    key_ids = jnp.arange(key_count, dtype=jnp.int32)
    query_ids = jnp.arange(query_count, dtype=jnp.int32)
    row_gap = (key_ids // ext_cols)[None, :] - (query_ids // sector_cols)[:, None]
    col_gap = (key_ids % ext_cols)[None, :] - (query_ids % sector_cols)[:, None]
    key_rows = row_first - radius + key_ids // ext_cols
    allowed = (
        (row_gap >= 0)
        & (row_gap < window_span)
        & (col_gap >= 0)
        & (col_gap < window_span)
        & ((key_rows >= 0) & (key_rows < total_rows))[None, :]
    )
    head_count = feature_width // HD
    group_size = math.gcd(head_count, 4)
    out_groups = []
    tan_groups = []
    for group_index in range(head_count // group_size):
        low_col = group_index * group_size * HD
        high_col = low_col + group_size * HD
        q_part = query_flat[:, low_col:high_col].reshape(query_count, group_size, HD)
        qt_part = qtan_flat[:, low_col:high_col].reshape(query_count, group_size, HD)
        k_part = keys_flat[0][:, low_col:high_col].reshape(key_count, group_size, HD)
        kt_part = keys_flat[1][:, low_col:high_col].reshape(key_count, group_size, HD)
        v_part = keys_flat[2][:, low_col:high_col].reshape(key_count, group_size, HD)
        vt_part = keys_flat[3][:, low_col:high_col].reshape(key_count, group_size, HD)
        scores = (
            jnp.einsum("qhd,khd->hqk", q_part, k_part, preferred_element_type=jnp.float32)
            * score_scale
        )
        scores = jnp.where(allowed[None], scores, -1e30)
        row_top = jnp.max(scores, axis=-1, keepdims=True)
        exp_scores = jnp.exp(scores - row_top)
        attention = exp_scores / jnp.sum(exp_scores, axis=-1, keepdims=True)
        slopes = (
            jnp.einsum("qhd,khd->hqk", qt_part, k_part, preferred_element_type=jnp.float32)
            + jnp.einsum("qhd,khd->hqk", q_part, kt_part, preferred_element_type=jnp.float32)
        ) * score_scale
        mean_slope = jnp.sum(attention * slopes, axis=-1, keepdims=True)
        weight_b = (attention * (slopes - mean_slope)).astype(jnp.bfloat16)
        prob_b = attention.astype(jnp.bfloat16)
        group_out = jnp.einsum("hqk,khd->qhd", prob_b, v_part, preferred_element_type=jnp.float32)
        group_tan = jnp.einsum(
            "hqk,khd->qhd", weight_b, v_part, preferred_element_type=jnp.float32
        ) + jnp.einsum("hqk,khd->qhd", prob_b, vt_part, preferred_element_type=jnp.float32)
        out_groups.append(group_out.reshape(query_count, group_size * HD))
        tan_groups.append(group_tan.reshape(query_count, group_size * HD))
    attended = jnp.concatenate(out_groups, axis=1).astype(jnp.bfloat16)
    attended_tan = jnp.concatenate(tan_groups, axis=1).astype(jnp.bfloat16)
    return (
        attended.reshape(band_rows, sector_cols, feature_width),
        attended_tan.reshape(band_rows, sector_cols, feature_width),
    )


BF = jnp.bfloat16
F32 = jnp.float32
MESH = pl.DeviceIdType.MESH


def ray_tables(total_rows, total_cols):
    quarter = HD // 4
    freq = (np.arange(quarter) + 1).astype(np.float32)
    rows = np.arange(total_rows).astype(np.float32)
    cols = np.arange(total_cols).astype(np.float32)
    lat = ((rows + np.float32(0.5)) * np.float32(math.pi / total_rows))[:, None] * freq[None, :]
    lon = (cols * np.float32(2.0 * math.pi / total_cols))[:, None] * freq[None, :]

    def table(fn, angle, first):
        part = fn(angle.astype(np.float64)).astype(np.float32)
        none = np.zeros_like(part)
        return np.concatenate([part, part, none, none] if first else [none, none, part, part], axis=1)

    row_tab = np.stack([table(np.cos, lat, True), table(np.sin, lat, True)])
    col_tab = np.stack([table(np.cos, lon, False), table(np.sin, lon, False)])
    return row_tab, col_tab


def kernel(
    n, n_lon, hp, band,
    q_ref, k_ref, v_ref, qt_ref, kt_ref, vt_ref, row_hbm, col_hbm,
    both_ref,
    raw_kv, raw_q, kvb, hs, outs, turn, bias, row_tab, col_tab,
    kv_send, kv_recv, q_send, q_recv, h_send, h_recv, o_send, o_recv, t_loc, greet, near, peers,
):
    me = lax.axis_index("lat")
    lon = lax.axis_index("lon")
    left = lax.rem(lon + n_lon - 1, n_lon)
    right = lax.rem(lon + 1, n_lon)
    cols = 16
    total = n * band
    pairs = total // 2

    def told(sem, lat, sector):
        pl.semaphore_signal(sem, inc=1, device_id=(lat, sector), device_id_type=MESH)

    barrier = pltpu.get_barrier_semaphore()
    lead, late = me == 0, me == n - 1
    middle = jnp.logical_not(jnp.logical_or(lead, late))
    first, last = lon == 0, lon == n_lon - 1
    odd = lax.rem(lon, 2) == 1
    middle_odd = jnp.logical_and(odd, jnp.logical_not(last))
    middle_even = jnp.logical_and(jnp.logical_not(odd), jnp.logical_not(first))

    @pl.when(lead)
    def _():
        for d in range(1, n):
            told(barrier, d, lon)

    @pl.when(middle)
    def _():
        told(barrier, 0, lon)
        told(barrier, n - 1, lon)

    @pl.when(jnp.logical_and(lead, jnp.logical_or(odd, first)))
    def _():
        told(barrier, me, left)

    @pl.when(jnp.logical_and(lead, middle_odd))
    def _():
        told(barrier, me, right)

    kv_refs = (k_ref, kt_ref, v_ref, vt_ref)
    q_refs = (q_ref, qt_ref)
    parts = tuple((j, 1) for j in range(hp))
    order = (0, *range(n - 2, 0, -1), n - 1)

    def taken(ref, sem):
        pltpu.make_async_copy(ref, ref, sem).wait()

    def lanes(owner, j, count):
        return pl.ds(pl.multiple_of((owner * hp + j) * HD, HD), count * HD)

    def kv_copy(a, p, peer):
        j, count = parts[p]
        return pltpu.make_async_remote_copy(
            src_ref=kv_refs[a].at[:, :, lanes(peer, j, count)],
            dst_ref=raw_kv.at[a, pl.ds(me * band, band), :, j * HD:(j + count) * HD],
            send_sem=kv_send,
            recv_sem=kv_recv.at[p, a],
            device_id=(peer, lon),
            device_id_type=MESH,
        )

    def q_copy(a, j, peer):
        return pltpu.make_async_remote_copy(
            src_ref=q_refs[a].at[:, :, lanes(peer, j, 1)],
            dst_ref=raw_q.at[j, a, pl.ds(me * band, band)],
            send_sem=q_send,
            recv_sem=q_recv.at[j],
            device_id=(peer, lon),
            device_id_type=MESH,
        )

    def own_q(a, j):
        return pltpu.make_async_copy(
            q_refs[a].at[:, :, lanes(me, j, 1)],
            raw_q.at[j, a, pl.ds(me * band, band)],
            q_recv.at[j],
        )

    def own_copy(a, p):
        j, count = parts[p]
        return pltpu.make_async_copy(
            kv_refs[a].at[:, :, lanes(me, j, count)],
            raw_kv.at[a, pl.ds(me * band, band), :, j * HD:(j + count) * HD],
            kv_recv.at[p, a],
        )

    halos = [(p, slice(0, 4)) for p in range(hp - 1)] + [(hp - 1, slice(a, a + 1)) for a in range(4)]

    def halo_copy(side, h):
        p, arrays = halos[h]
        j, count = parts[p]
        return pltpu.make_async_remote_copy(
            src_ref=hs.at[side, arrays, j:j + count],
            dst_ref=kvb.at[arrays, j:j + count, :, 3 - side],
            send_sem=h_send,
            recv_sem=h_recv.at[p],
            device_id=(me, right if side else left),
            device_id_type=MESH,
        )

    def out_copy(j, d):
        peer = lax.rem(me + d, n)
        return pltpu.make_async_remote_copy(
            src_ref=outs.at[j, :, pl.ds(peer * band, band)],
            dst_ref=both_ref.at[:, :, :, lanes(me, j, 1)],
            send_sem=o_send,
            recv_sem=o_recv,
            device_id=(peer, lon),
            device_id_type=MESH,
        )

    def own_out(j):
        return pltpu.make_async_copy(
            outs.at[j, :, pl.ds(me * band, band)],
            both_ref.at[:, :, :, lanes(me, j, 1)],
            o_recv,
        )

    def send_out(j, b):
        @pl.when(me == b)
        def _():
            own_out(j).start()

        @pl.when(me != b)
        def _():
            out_copy(j, lax.rem(b - me + n, n)).start()

    here = pl.ds(pl.multiple_of(lon * cols, cols), cols)
    row_copy = pltpu.make_async_copy(row_hbm, row_tab, t_loc.at[0])
    col_copy = pltpu.make_async_copy(col_hbm.at[:, here], col_tab, t_loc.at[1])
    row_copy.start()
    col_copy.start()

    @pl.when(late)
    def _():
        pl.semaphore_wait(barrier, n - 1)
        for d in range(n - 1):
            told(peers, d, lon)

    @pl.when(middle)
    def _():
        pl.semaphore_wait(barrier, 1)

    @pl.when(jnp.logical_and(lead, middle_odd))
    def _():
        pl.semaphore_wait(barrier, n - 2)

    @pl.when(jnp.logical_and(lead, middle_even))
    def _():
        pl.semaphore_wait(barrier, n)

    @pl.when(jnp.logical_and(lead, jnp.logical_or(first, last)))
    def _():
        pl.semaphore_wait(barrier, n - 1)

    @pl.when(jnp.logical_not(lead))
    def _():
        for a in range(4):
            kv_copy(a, 0, 0).start()

    @pl.when(lead)
    def _():
        for d in range(1, n - 1):
            for a in range(4):
                kv_copy(a, 0, d).start()

    @pl.when(jnp.logical_not(late))
    def _():
        pl.semaphore_wait(peers, 1)

    @pl.when(jnp.logical_and(lead, middle_even))
    def _():
        told(near.at[1], me, left)
        told(near.at[0], me, right)

    @pl.when(jnp.logical_and(lead, jnp.logical_or(first, last)))
    def _():
        told(near.at[0], me, right)

    @pl.when(lead)
    def _():
        for a in range(4):
            kv_copy(a, 0, n - 1).start()

    for peer in order[1:]:
        @pl.when(jnp.logical_not(jnp.logical_or(lead, peer == me)))
        def _():
            for a in range(4):
                kv_copy(a, 0, peer).start()

    for a in range(4):
        own_copy(a, 0).start()
    for p in range(1, len(parts)):
        for peer in order:
            @pl.when(peer != me)
            def _():
                for a in range(4):
                    kv_copy(a, p, peer).start()

        for a in range(4):
            own_copy(a, p).start()
    for j in range(hp):
        for peer in order:
            @pl.when(peer != me)
            def _():
                for a in range(2):
                    q_copy(a, j, peer).start()

        for a in range(2):
            own_q(a, j).start()

    row_copy.wait()
    col_copy.wait()
    for t in range(2):
        whole = row_tab[t][:, None, :] + col_tab[t][None, :, :]
        turn[t] = whole.reshape(total * cols, HD)
    shape = (band * cols, (band + WIN) * 2 * cols)
    query = lax.broadcasted_iota(jnp.int32, shape, 0)
    key = lax.broadcasted_iota(jnp.int32, shape, 1)
    part = (key % 64) // 16
    spot = key % 16
    own = part < 2
    key_row = (key // 64) * 2 + jnp.where(own, part, spot // 8)
    key_col = jnp.where(own, spot, jnp.where(part == 2, spot % 8 - 8, spot % 8 + 16))
    row_gap = key_row - query // 16
    col_gap = key_col - query % 16 + WIN // 2
    allowed = (row_gap >= 0) & (row_gap < WIN) & (col_gap >= 0) & (col_gap < WIN)
    bias[...] = jnp.where(allowed, 0.0, -1e30)
    src = lax.broadcasted_iota(jnp.int32, (HD, HD), 0)
    dst = lax.broadcasted_iota(jnp.int32, (HD, HD), 1)
    low = (dst % 64) < 32
    swap = (
        jnp.where(low & (src == dst + 32), -1.0, 0.0)
        + jnp.where(jnp.logical_not(low) & (src == dst - 32), 1.0, 0.0)
    ).astype(BF)

    def turned(x):
        flat = x.reshape(total * cols, HD)
        other = jnp.dot(flat, swap, preferred_element_type=F32)
        return flat.astype(F32) * turn[0] + other * turn[1]

    def stage(a, j):
        x = raw_kv[a, :, :, pl.ds(pl.multiple_of(j * HD, HD), HD)]
        y = turned(x) if a < 2 else x.reshape(total * cols, HD).astype(F32)
        kvb[a, j, :, 0:2] = y.reshape(pairs, 2, cols, HD).astype(BF)
        halves = y.reshape(total, 2, cols // 2, HD)
        for side in range(2):
            hs[side, a, j] = halves[:, side].reshape(pairs, cols, HD).astype(BF)

    @pl.when(lead)
    def _():
        pl.semaphore_wait(near.at[0], 1)

        @pl.when(jnp.logical_or(middle_odd, last))
        def _():
            told(near.at[1], me, left)

        pl.semaphore_wait(near.at[1], 1)

        @pl.when(middle_odd)
        def _():
            told(near.at[0], me, right)

        @pl.when(first)
        def _():
            told(near.at[1], me, left)

        for d in range(1, n):
            told(greet, lax.rem(me + d, n), lon)

    for p in range(len(parts)):
        for a in range(4):
            j, count = parts[p]
            taken(raw_kv.at[a, :, :, j * HD:(j + count) * HD], kv_recv.at[p, a])
            if parts[p][1] == 1:
                stage(a, parts[p][0])
            else:
                pl.loop(parts[p][0], sum(parts[p]))(functools.partial(stage, a))
            if p == 0 and a == 0:
                @pl.when(jnp.logical_not(lead))
                def _():
                    pl.semaphore_wait(greet, 1)

            for h in range(len(halos)):
                if halos[h][0] == p and halos[h][1].stop == a + 1:
                    for side in range(2):
                        halo_copy(side, h).start()

    scale2 = math.log2(math.e) / math.sqrt(HD)
    scale = 1.0 / math.sqrt(HD)

    @pl.loop(0, hp)
    def _(j):
        for p in range(len(parts)):
            @pl.when(j == parts[p][0])
            def _():
                taken(kvb.at[:, parts[p][0]:sum(parts[p]), :, 2:4], h_recv.at[p])

        taken(raw_q.at[j], q_recv.at[j])
        for a in range(2):
            raw_q[j, a] = turned(raw_q[j, a]).astype(BF).reshape(total, cols, HD)
        nq = band * cols
        for b in order:
            first = max(0, b * band - WIN // 2)
            last = min(total, (b + 1) * band + WIN // 2)
            skip = (first - (b * band - WIN // 2)) // 2 * 64
            p0, p1 = first // 2, last // 2
            nk = (p1 - p0) * 64
            keys = kvb[0, j, p0:p1].reshape(nk, HD)
            ktan = kvb[1, j, p0:p1].reshape(nk, HD)
            val = kvb[2, j, p0:p1].reshape(nk, HD)
            vtan = kvb[3, j, p0:p1].reshape(nk, HD)
            rows = slice(b * band, (b + 1) * band)
            q = raw_q[j, 0, rows].reshape(nq, HD)
            qt = raw_q[j, 1, rows].reshape(nq, HD)
            nt = (((1,), (1,)), ((), ()))
            score = lax.dot_general(q, keys, nt, preferred_element_type=F32)
            score = score * scale2 + bias[:, skip:skip + nk]
            top = jnp.max(score, axis=-1, keepdims=True)
            e = jnp.exp2(score - top)
            inv = 1.0 / jnp.sum(e, axis=-1, keepdims=True)
            slope = lax.dot_general(
                jnp.concatenate([qt, q], axis=1),
                jnp.concatenate([keys, ktan], axis=1),
                nt,
                preferred_element_type=F32,
            )
            mean = jnp.sum(e * slope, axis=-1, keepdims=True) * inv
            prob = e * inv
            prob_b = prob.astype(BF)
            weight_b = (prob * ((slope - mean) * scale)).astype(BF)
            both = jnp.dot(
                prob_b, jnp.concatenate([val, vtan], axis=1), preferred_element_type=F32
            )
            tan = both[:, HD:] + jnp.dot(weight_b, val, preferred_element_type=F32)
            outs[j, 0, rows] = both[:, :HD].astype(BF).reshape(band, cols, HD)
            outs[j, 1, rows] = tan.astype(BF).reshape(band, cols, HD)

            @pl.when(jnp.logical_not(odd))
            def _():
                send_out(j, b)

        @pl.when(odd)
        def _():
            for b in order:
                send_out(j, b)

    taken(raw_kv.at[:, 0:total - band], kv_send)
    taken(raw_q.at[:, :, 0:total - band], q_send)
    taken(hs, h_send)
    taken(outs.at[:, :, 0:total - band], o_send)
    taken(both_ref, o_recv)


def shards(mesh_shape, *args):
    band, cols, width = args[0].shape
    n, n_lon = mesh_shape["lat"], mesh_shape["lon"]
    heads = width // HD
    fits = (
        heads % n == 0 and n > 1 and n_lon > 2 and n_lon % 2 == 0
        and cols == WIN and band == WIN // 2
    )
    if not fits:
        return shards_halo(*args)
    hp = heads // n
    total = band * n
    row_tab, col_tab = ray_tables(total, cols * n_lon)
    hbm = pl.BlockSpec(memory_space=pltpu.HBM)
    anywhere = pl.BlockSpec(memory_space=pl.ANY)
    q, k, v, qt, kt, vt = args
    dma = pltpu.SemaphoreType.DMA
    nq = band * cols
    nk = (band + WIN) * 2 * cols
    both = pl.pallas_call(
        functools.partial(kernel, n, n_lon, hp, band),
        out_shape=pltpu.VMEM((2, band, cols, width), BF),
        in_specs=[hbm] * 8,
        out_specs=anywhere,
        scratch_shapes=[
            pltpu.VMEM((4, total, cols, hp * HD), BF),
            pltpu.VMEM((hp, 2, total, cols, HD), BF),
            pltpu.VMEM((4, hp, total // 2, 4, cols, HD), BF),
            pltpu.VMEM((2, 4, hp, total // 2, cols, HD), BF),
            pltpu.VMEM((hp, 2, total, cols, HD), BF),
            pltpu.VMEM((2, total * cols, HD), F32),
            pltpu.VMEM((nq, nk), F32),
            pltpu.VMEM((2, total, HD), F32),
            pltpu.VMEM((2, cols, HD), F32),
            dma,
            dma((hp, 4)),
            dma,
            dma((hp,)),
            dma,
            dma((hp,)),
            dma,
            dma,
            dma((2,)),
            pltpu.SemaphoreType.REGULAR,
            pltpu.SemaphoreType.REGULAR((2,)),
            pltpu.SemaphoreType.REGULAR,
        ],
        compiler_params=pltpu.CompilerParams(
            collective_id=0, has_side_effects=True, vmem_limit_bytes=60 * 1024 * 1024
        ),
        name="panorama",
    )(q, k, v, qt, kt, vt, jnp.asarray(row_tab), jnp.asarray(col_tab))
    return both[0], both[1]


def solution(mesh):
    placed = (
        P("lat", "lon", None),
        P("lat", "lon", None),
        P("lat", "lon", None),
        P("lat", "lon", None),
        P("lat", "lon", None),
        P("lat", "lon", None),
    )
    return jax.shard_map(
        functools.partial(shards, dict(mesh.shape)),
        mesh=mesh,
        in_specs=placed,
        out_specs=(P("lat", "lon", None), P("lat", "lon", None)),
        check_vma=False,
    )
```

```python
import functools
import math

import jax
import jax.numpy as jnp
import numpy as np
from jax import lax
from jax.experimental import pallas as pl
from jax.experimental.pallas import tpu as pltpu
from jax.sharding import PartitionSpec as P

HD = 128
WIN = 16


def extended_2(shard, sides, width, wrap):
    for axis, dim in sides:
        count, length = (lax.axis_size(axis), shard.shape[dim])
        up = [(i, (i + 1) % count) for i in range(count if wrap else count - 1)]
        down = [(j, i) for i, j in up]
        last = lax.slice_in_dim(shard, length - width, length, axis=dim)
        leading = lax.slice_in_dim(shard, 0, width, axis=dim)
        before = lax.ppermute(last, axis, up)
        after = lax.ppermute(leading, axis, down)
        shard = jnp.concatenate([before, shard, after], axis=dim)
    return shard


def rotate_rays(values, row_first, col_first, total_rows, total_cols):
    band_rows, sector_cols, feature_width = values.shape
    quarter = HD // 4
    head_count = feature_width // HD
    frequency = (jnp.arange(quarter, dtype=jnp.int32) + 1).astype(jnp.float32)
    row_ids = (row_first + jnp.arange(band_rows, dtype=jnp.int32)).astype(jnp.float32)
    col_ids = (col_first + jnp.arange(sector_cols, dtype=jnp.int32)).astype(jnp.float32)
    lat_angle = ((row_ids + 0.5) * (math.pi / total_rows))[:, None] * frequency[None, :]
    lon_angle = (col_ids * (2.0 * math.pi / total_cols))[:, None] * frequency[None, :]
    lat_cos = jnp.cos(lat_angle)[:, None, None, :]
    lat_sin = jnp.sin(lat_angle)[:, None, None, :]
    lon_cos = jnp.cos(lon_angle)[None, :, None, :]
    lon_sin = jnp.sin(lon_angle)[None, :, None, :]
    quarters = values.astype(jnp.float32).reshape(band_rows, sector_cols, head_count, 4, quarter)
    lat_one = quarters[:, :, :, 0, :]
    lat_two = quarters[:, :, :, 1, :]
    lon_one = quarters[:, :, :, 2, :]
    lon_two = quarters[:, :, :, 3, :]
    turned = jnp.stack(
        [
            lat_one * lat_cos - lat_two * lat_sin,
            lat_one * lat_sin + lat_two * lat_cos,
            lon_one * lon_cos - lon_two * lon_sin,
            lon_one * lon_sin + lon_two * lon_cos,
        ],
        axis=3,
    )
    return turned.reshape(band_rows, sector_cols, feature_width).astype(jnp.bfloat16)


def widen_rows(stacked, radius):
    padded = extended_2(stacked, (("lat", 1),), radius, False)
    return padded[:, : padded.shape[1] - 1]


def widen_cols(stacked, radius):
    padded = extended_2(stacked, (("lon", 2),), radius, True)
    return padded[:, :, : padded.shape[2] - 1]


def shards_halo(query_tok, key_tok, value_tok, query_tan, key_tan, value_tan):
    band_rows, sector_cols, feature_width = query_tok.shape
    radius = WIN // 2
    window_span = 2 * radius
    score_scale = 1.0 / math.sqrt(HD)
    total_rows = band_rows * lax.axis_size("lat")
    total_cols = sector_cols * lax.axis_size("lon")
    row_first = lax.axis_index("lat") * band_rows
    col_first = lax.axis_index("lon") * sector_cols
    rot_query = rotate_rays(query_tok, row_first, col_first, total_rows, total_cols)
    rot_qtan = rotate_rays(query_tan, row_first, col_first, total_rows, total_cols)
    rot_key = rotate_rays(key_tok, row_first, col_first, total_rows, total_cols)
    rot_ktan = rotate_rays(key_tan, row_first, col_first, total_rows, total_cols)
    stacked = jnp.stack([rot_key, rot_ktan, value_tok, value_tan])
    extended = widen_rows(widen_cols(stacked, radius), radius)
    ext_rows = band_rows + window_span - 1
    ext_cols = sector_cols + window_span - 1
    key_count = ext_rows * ext_cols
    query_count = band_rows * sector_cols
    keys_flat = extended.reshape(4, key_count, feature_width)
    query_flat = rot_query.reshape(query_count, feature_width)
    qtan_flat = rot_qtan.reshape(query_count, feature_width)
    key_ids = jnp.arange(key_count, dtype=jnp.int32)
    query_ids = jnp.arange(query_count, dtype=jnp.int32)
    row_gap = (key_ids // ext_cols)[None, :] - (query_ids // sector_cols)[:, None]
    col_gap = (key_ids % ext_cols)[None, :] - (query_ids % sector_cols)[:, None]
    key_rows = row_first - radius + key_ids // ext_cols
    allowed = (
        (row_gap >= 0)
        & (row_gap < window_span)
        & (col_gap >= 0)
        & (col_gap < window_span)
        & ((key_rows >= 0) & (key_rows < total_rows))[None, :]
    )
    head_count = feature_width // HD
    group_size = math.gcd(head_count, 4)
    out_groups = []
    tan_groups = []
    for group_index in range(head_count // group_size):
        low_col = group_index * group_size * HD
        high_col = low_col + group_size * HD
        q_part = query_flat[:, low_col:high_col].reshape(query_count, group_size, HD)
        qt_part = qtan_flat[:, low_col:high_col].reshape(query_count, group_size, HD)
        k_part = keys_flat[0][:, low_col:high_col].reshape(key_count, group_size, HD)
        kt_part = keys_flat[1][:, low_col:high_col].reshape(key_count, group_size, HD)
        v_part = keys_flat[2][:, low_col:high_col].reshape(key_count, group_size, HD)
        vt_part = keys_flat[3][:, low_col:high_col].reshape(key_count, group_size, HD)
        scores = (
            jnp.einsum("qhd,khd->hqk", q_part, k_part, preferred_element_type=jnp.float32)
            * score_scale
        )
        scores = jnp.where(allowed[None], scores, -1e30)
        row_top = jnp.max(scores, axis=-1, keepdims=True)
        exp_scores = jnp.exp(scores - row_top)
        attention = exp_scores / jnp.sum(exp_scores, axis=-1, keepdims=True)
        slopes = (
            jnp.einsum("qhd,khd->hqk", qt_part, k_part, preferred_element_type=jnp.float32)
            + jnp.einsum("qhd,khd->hqk", q_part, kt_part, preferred_element_type=jnp.float32)
        ) * score_scale
        mean_slope = jnp.sum(attention * slopes, axis=-1, keepdims=True)
        weight_b = (attention * (slopes - mean_slope)).astype(jnp.bfloat16)
        prob_b = attention.astype(jnp.bfloat16)
        group_out = jnp.einsum("hqk,khd->qhd", prob_b, v_part, preferred_element_type=jnp.float32)
        group_tan = jnp.einsum(
            "hqk,khd->qhd", weight_b, v_part, preferred_element_type=jnp.float32
        ) + jnp.einsum("hqk,khd->qhd", prob_b, vt_part, preferred_element_type=jnp.float32)
        out_groups.append(group_out.reshape(query_count, group_size * HD))
        tan_groups.append(group_tan.reshape(query_count, group_size * HD))
    attended = jnp.concatenate(out_groups, axis=1).astype(jnp.bfloat16)
    attended_tan = jnp.concatenate(tan_groups, axis=1).astype(jnp.bfloat16)
    return (
        attended.reshape(band_rows, sector_cols, feature_width),
        attended_tan.reshape(band_rows, sector_cols, feature_width),
    )


BF = jnp.bfloat16
F32 = jnp.float32
MESH = pl.DeviceIdType.MESH


def ray_tables(total_rows, total_cols):
    quarter = HD // 4
    freq = (np.arange(quarter) + 1).astype(np.float32)
    rows = np.arange(total_rows).astype(np.float32)
    cols = np.arange(total_cols).astype(np.float32)
    lat = ((rows + np.float32(0.5)) * np.float32(math.pi / total_rows))[:, None] * freq[None, :]
    lon = (cols * np.float32(2.0 * math.pi / total_cols))[:, None] * freq[None, :]

    def table(fn, angle, first):
        part = fn(angle.astype(np.float64)).astype(np.float32)
        none = np.zeros_like(part)
        return np.concatenate([part, part, none, none] if first else [none, none, part, part], axis=1)

    row_tab = np.stack([table(np.cos, lat, True), table(np.sin, lat, True)])
    col_tab = np.stack([table(np.cos, lon, False), table(np.sin, lon, False)])
    return row_tab, col_tab


def kernel(
    n, n_lon, hp, band,
    q_ref, k_ref, v_ref, qt_ref, kt_ref, vt_ref, row_hbm, col_hbm,
    both_ref,
    raw_kv, raw_q, kvb, hs, outs, turn, bias, row_tab, col_tab,
    kv_send, kv_recv, q_send, q_recv, h_send, h_recv, o_send, o_recv, t_loc, greet, near, peers,
):
    me = lax.axis_index("lat")
    lon = lax.axis_index("lon")
    left = lax.rem(lon + n_lon - 1, n_lon)
    right = lax.rem(lon + 1, n_lon)
    cols = 16
    total = n * band
    pairs = total // 2

    def told(sem, lat, sector):
        pl.semaphore_signal(sem, inc=1, device_id=(lat, sector), device_id_type=MESH)

    barrier = pltpu.get_barrier_semaphore()
    lead, late = me == 0, me == n - 1
    middle = jnp.logical_not(jnp.logical_or(lead, late))
    first, last = lon == 0, lon == n_lon - 1
    odd = lax.rem(lon, 2) == 1
    middle_odd = jnp.logical_and(odd, jnp.logical_not(last))
    middle_even = jnp.logical_and(jnp.logical_not(odd), jnp.logical_not(first))

    @pl.when(lead)
    def _():
        for d in range(1, n):
            told(barrier, d, lon)

    @pl.when(middle)
    def _():
        told(barrier, 0, lon)
        told(barrier, n - 1, lon)

    @pl.when(jnp.logical_and(lead, jnp.logical_or(odd, first)))
    def _():
        told(barrier, me, left)

    @pl.when(jnp.logical_and(lead, middle_odd))
    def _():
        told(barrier, me, right)

    kv_refs = (k_ref, kt_ref, v_ref, vt_ref)
    q_refs = (q_ref, qt_ref)
    parts = tuple((j, 1) for j in range(hp))
    order = (0, *range(n - 2, 0, -1), n - 1)

    def taken(ref, sem):
        pltpu.make_async_copy(ref, ref, sem).wait()

    def lanes(owner, j, count):
        return pl.ds(pl.multiple_of((owner * hp + j) * HD, HD), count * HD)

    def kv_copy(a, p, peer):
        j, count = parts[p]
        return pltpu.make_async_remote_copy(
            src_ref=kv_refs[a].at[:, :, lanes(peer, j, count)],
            dst_ref=raw_kv.at[a, pl.ds(me * band, band), :, j * HD:(j + count) * HD],
            send_sem=kv_send,
            recv_sem=kv_recv.at[p, a],
            device_id=(peer, lon),
            device_id_type=MESH,
        )

    def q_copy(a, j, peer):
        return pltpu.make_async_remote_copy(
            src_ref=q_refs[a].at[:, :, lanes(peer, j, 1)],
            dst_ref=raw_q.at[j, a, pl.ds(me * band, band)],
            send_sem=q_send,
            recv_sem=q_recv.at[j],
            device_id=(peer, lon),
            device_id_type=MESH,
        )

    def own_q(a, j):
        return pltpu.make_async_copy(
            q_refs[a].at[:, :, lanes(me, j, 1)],
            raw_q.at[j, a, pl.ds(me * band, band)],
            q_recv.at[j],
        )

    def own_copy(a, p):
        j, count = parts[p]
        return pltpu.make_async_copy(
            kv_refs[a].at[:, :, lanes(me, j, count)],
            raw_kv.at[a, pl.ds(me * band, band), :, j * HD:(j + count) * HD],
            kv_recv.at[p, a],
        )

    halos = [(p, slice(0, 4)) for p in range(hp - 1)] + [(hp - 1, slice(a, a + 1)) for a in range(4)]

    def halo_copy(side, h):
        p, arrays = halos[h]
        j, count = parts[p]
        return pltpu.make_async_remote_copy(
            src_ref=hs.at[side, arrays, j:j + count],
            dst_ref=kvb.at[arrays, j:j + count, :, 3 - side],
            send_sem=h_send,
            recv_sem=h_recv.at[p],
            device_id=(me, right if side else left),
            device_id_type=MESH,
        )

    def out_copy(j, d):
        peer = lax.rem(me + d, n)
        return pltpu.make_async_remote_copy(
            src_ref=outs.at[j, :, pl.ds(peer * band, band)],
            dst_ref=both_ref.at[:, :, :, lanes(me, j, 1)],
            send_sem=o_send,
            recv_sem=o_recv,
            device_id=(peer, lon),
            device_id_type=MESH,
        )

    def own_out(j):
        return pltpu.make_async_copy(
            outs.at[j, :, pl.ds(me * band, band)],
            both_ref.at[:, :, :, lanes(me, j, 1)],
            o_recv,
        )

    def send_out(j, b):
        @pl.when(me == b)
        def _():
            own_out(j).start()

        @pl.when(me != b)
        def _():
            out_copy(j, lax.rem(b - me + n, n)).start()

    here = pl.ds(pl.multiple_of(lon * cols, cols), cols)
    row_copy = pltpu.make_async_copy(row_hbm, row_tab, t_loc.at[0])
    col_copy = pltpu.make_async_copy(col_hbm.at[:, here], col_tab, t_loc.at[1])
    row_copy.start()
    col_copy.start()

    @pl.when(late)
    def _():
        pl.semaphore_wait(barrier, n - 1)
        for d in range(n - 1):
            told(peers, d, lon)

    @pl.when(middle)
    def _():
        pl.semaphore_wait(barrier, 1)

    @pl.when(jnp.logical_and(lead, middle_odd))
    def _():
        pl.semaphore_wait(barrier, n - 2)

    @pl.when(jnp.logical_and(lead, middle_even))
    def _():
        pl.semaphore_wait(barrier, n)

    @pl.when(jnp.logical_and(lead, jnp.logical_or(first, last)))
    def _():
        pl.semaphore_wait(barrier, n - 1)

    @pl.when(jnp.logical_not(lead))
    def _():
        for a in range(4):
            kv_copy(a, 0, 0).start()

    @pl.when(lead)
    def _():
        for d in range(1, n - 1):
            for a in range(4):
                kv_copy(a, 0, d).start()

    @pl.when(jnp.logical_not(late))
    def _():
        pl.semaphore_wait(peers, 1)

    @pl.when(jnp.logical_and(lead, middle_even))
    def _():
        told(near.at[1], me, left)
        told(near.at[0], me, right)

    @pl.when(jnp.logical_and(lead, jnp.logical_or(first, last)))
    def _():
        told(near.at[0], me, right)

    @pl.when(lead)
    def _():
        for a in range(4):
            kv_copy(a, 0, n - 1).start()

    for peer in order[1:]:
        @pl.when(jnp.logical_not(jnp.logical_or(lead, peer == me)))
        def _():
            for a in range(4):
                kv_copy(a, 0, peer).start()

    for a in range(4):
        own_copy(a, 0).start()
    for p in range(1, len(parts)):
        for peer in order:
            @pl.when(peer != me)
            def _():
                for a in range(4):
                    kv_copy(a, p, peer).start()

        for a in range(4):
            own_copy(a, p).start()
    for j in range(hp):
        for peer in order:
            @pl.when(peer != me)
            def _():
                for a in range(2):
                    q_copy(a, j, peer).start()

        for a in range(2):
            own_q(a, j).start()

    row_copy.wait()
    col_copy.wait()
    for t in range(2):
        whole = row_tab[t][:, None, :] + col_tab[t][None, :, :]
        turn[t] = whole.reshape(total * cols, HD)
    shape = (band * cols, (band + WIN) * 2 * cols)
    query = lax.broadcasted_iota(jnp.int32, shape, 0)
    key = lax.broadcasted_iota(jnp.int32, shape, 1)
    part = (key % 64) // 16
    spot = key % 16
    own = part < 2
    key_row = (key // 64) * 2 + jnp.where(own, part, spot // 8)
    key_col = jnp.where(own, spot, jnp.where(part == 2, spot % 8 - 8, spot % 8 + 16))
    row_gap = key_row - query // 16
    col_gap = key_col - query % 16 + WIN // 2
    allowed = (row_gap >= 0) & (row_gap < WIN) & (col_gap >= 0) & (col_gap < WIN)
    bias[...] = jnp.where(allowed, 0.0, -1e30)
    src = lax.broadcasted_iota(jnp.int32, (HD, HD), 0)
    dst = lax.broadcasted_iota(jnp.int32, (HD, HD), 1)
    low = (dst % 64) < 32
    swap = (
        jnp.where(low & (src == dst + 32), -1.0, 0.0)
        + jnp.where(jnp.logical_not(low) & (src == dst - 32), 1.0, 0.0)
    ).astype(BF)

    def turned(x):
        flat = x.reshape(total * cols, HD)
        other = jnp.dot(flat, swap, preferred_element_type=F32)
        return flat.astype(F32) * turn[0] + other * turn[1]

    def stage(a, j):
        x = raw_kv[a, :, :, pl.ds(pl.multiple_of(j * HD, HD), HD)]
        y = turned(x) if a < 2 else x.reshape(total * cols, HD).astype(F32)
        kvb[a, j, :, 0:2] = y.reshape(pairs, 2, cols, HD).astype(BF)
        halves = y.reshape(total, 2, cols // 2, HD)
        for side in range(2):
            hs[side, a, j] = halves[:, side].reshape(pairs, cols, HD).astype(BF)

    @pl.when(lead)
    def _():
        pl.semaphore_wait(near.at[0], 1)

        @pl.when(jnp.logical_or(middle_odd, last))
        def _():
            told(near.at[1], me, left)

        pl.semaphore_wait(near.at[1], 1)

        @pl.when(middle_odd)
        def _():
            told(near.at[0], me, right)

        @pl.when(first)
        def _():
            told(near.at[1], me, left)

        for d in range(1, n):
            told(greet, lax.rem(me + d, n), lon)

    for p in range(len(parts)):
        for a in range(4):
            j, count = parts[p]
            taken(raw_kv.at[a, :, :, j * HD:(j + count) * HD], kv_recv.at[p, a])
            if parts[p][1] == 1:
                stage(a, parts[p][0])
            else:
                pl.loop(parts[p][0], sum(parts[p]))(functools.partial(stage, a))
            if p == 0 and a == 0:
                @pl.when(jnp.logical_not(lead))
                def _():
                    pl.semaphore_wait(greet, 1)

            for h in range(len(halos)):
                if halos[h][0] == p and halos[h][1].stop == a + 1:
                    for side in range(2):
                        halo_copy(side, h).start()

    scale2 = math.log2(math.e) / math.sqrt(HD)
    scale = 1.0 / math.sqrt(HD)

    @pl.loop(0, hp)
    def _(j):
        for p in range(len(parts)):
            @pl.when(j == parts[p][0])
            def _():
                taken(kvb.at[:, parts[p][0]:sum(parts[p]), :, 2:4], h_recv.at[p])

        taken(raw_q.at[j], q_recv.at[j])
        for a in range(2):
            raw_q[j, a] = turned(raw_q[j, a]).astype(BF).reshape(total, cols, HD)
        nq = band * cols
        for b in order:
            first = max(0, b * band - WIN // 2)
            last = min(total, (b + 1) * band + WIN // 2)
            skip = (first - (b * band - WIN // 2)) // 2 * 64
            p0, p1 = first // 2, last // 2
            nk = (p1 - p0) * 64
            keys = kvb[0, j, p0:p1].reshape(nk, HD)
            ktan = kvb[1, j, p0:p1].reshape(nk, HD)
            val = kvb[2, j, p0:p1].reshape(nk, HD)
            vtan = kvb[3, j, p0:p1].reshape(nk, HD)
            rows = slice(b * band, (b + 1) * band)
            q = raw_q[j, 0, rows].reshape(nq, HD)
            qt = raw_q[j, 1, rows].reshape(nq, HD)
            nt = (((1,), (1,)), ((), ()))
            score = lax.dot_general(q, keys, nt, preferred_element_type=F32)
            score = score * scale2 + bias[:, skip:skip + nk]
            top = jnp.max(score, axis=-1, keepdims=True)
            e = jnp.exp2(score - top)
            inv = 1.0 / jnp.sum(e, axis=-1, keepdims=True)
            slope = lax.dot_general(
                jnp.concatenate([qt, q], axis=1),
                jnp.concatenate([keys, ktan], axis=1),
                nt,
                preferred_element_type=F32,
            )
            mean = jnp.sum(e * slope, axis=-1, keepdims=True) * inv
            prob = e * inv
            prob_b = prob.astype(BF)
            weight_b = (prob * ((slope - mean) * scale)).astype(BF)
            both = jnp.dot(
                prob_b, jnp.concatenate([val, vtan], axis=1), preferred_element_type=F32
            )
            tan = both[:, HD:] + jnp.dot(weight_b, val, preferred_element_type=F32)
            outs[j, 0, rows] = both[:, :HD].astype(BF).reshape(band, cols, HD)
            outs[j, 1, rows] = tan.astype(BF).reshape(band, cols, HD)

            @pl.when(jnp.logical_not(odd))
            def _():
                send_out(j, b)

        @pl.when(odd)
        def _():
            for b in order:
                send_out(j, b)

    taken(raw_kv.at[:, 0:total - band], kv_send)
    taken(raw_q.at[:, :, 0:total - band], q_send)
    taken(hs, h_send)
    taken(outs.at[:, :, 0:total - band], o_send)
    taken(both_ref, o_recv)


def spread(both_ref, out_ref, tan_ref, sems):
    copies = [
        pltpu.make_async_copy(both_ref.at[o], ref, sems.at[o])
        for o, ref in enumerate((out_ref, tan_ref))
    ]
    for copy in copies:
        copy.start()
    for copy in copies:
        copy.wait()


def shards(mesh_shape, *args):
    band, cols, width = args[0].shape
    n, n_lon = mesh_shape["lat"], mesh_shape["lon"]
    heads = width // HD
    fits = (
        heads % n == 0 and n > 1 and n_lon > 2 and n_lon % 2 == 0
        and cols == WIN and band == WIN // 2
    )
    if not fits:
        return shards_halo(*args)
    hp = heads // n
    total = band * n
    row_tab, col_tab = ray_tables(total, cols * n_lon)
    hbm = pl.BlockSpec(memory_space=pltpu.HBM)
    anywhere = pl.BlockSpec(memory_space=pl.ANY)
    q, k, v, qt, kt, vt = args
    dma = pltpu.SemaphoreType.DMA
    nq = band * cols
    nk = (band + WIN) * 2 * cols
    both = pl.pallas_call(
        functools.partial(kernel, n, n_lon, hp, band),
        out_shape=pltpu.VMEM((2, band, cols, width), BF),
        in_specs=[hbm] * 8,
        out_specs=anywhere,
        scratch_shapes=[
            pltpu.VMEM((4, total, cols, hp * HD), BF),
            pltpu.VMEM((hp, 2, total, cols, HD), BF),
            pltpu.VMEM((4, hp, total // 2, 4, cols, HD), BF),
            pltpu.VMEM((2, 4, hp, total // 2, cols, HD), BF),
            pltpu.VMEM((hp, 2, total, cols, HD), BF),
            pltpu.VMEM((2, total * cols, HD), F32),
            pltpu.VMEM((nq, nk), F32),
            pltpu.VMEM((2, total, HD), F32),
            pltpu.VMEM((2, cols, HD), F32),
            dma,
            dma((hp, 4)),
            dma,
            dma((hp,)),
            dma,
            dma((hp,)),
            dma,
            dma,
            dma((2,)),
            pltpu.SemaphoreType.REGULAR,
            pltpu.SemaphoreType.REGULAR((2,)),
            pltpu.SemaphoreType.REGULAR,
        ],
        compiler_params=pltpu.CompilerParams(
            collective_id=0, has_side_effects=True, vmem_limit_bytes=60 * 1024 * 1024
        ),
        name="panorama",
    )(q, k, v, qt, kt, vt, jnp.asarray(row_tab), jnp.asarray(col_tab))
    return tuple(
        pl.pallas_call(
            spread,
            out_shape=[jax.ShapeDtypeStruct((band, cols, width), BF)] * 2,
            in_specs=[anywhere],
            out_specs=[hbm] * 2,
            scratch_shapes=[dma((2,))],
            name="spread",
        )(pltpu.with_memory_space_constraint(both, pltpu.VMEM))
    )


def solution(mesh):
    placed = (
        P("lat", "lon", None),
        P("lat", "lon", None),
        P("lat", "lon", None),
        P("lat", "lon", None),
        P("lat", "lon", None),
        P("lat", "lon", None),
    )
    return jax.shard_map(
        functools.partial(shards, dict(mesh.shape)),
        mesh=mesh,
        in_specs=placed,
        out_specs=(P("lat", "lon", None), P("lat", "lon", None)),
        check_vma=False,
    )
```

```python
import functools
import math

import jax
import jax.numpy as jnp
import numpy as np
from jax import lax
from jax.experimental import pallas as pl
from jax.experimental.pallas import tpu as pltpu
from jax.sharding import PartitionSpec as P

HD = 128
WIN = 16


def extended_2(shard, sides, width, wrap):
    for axis, dim in sides:
        count, length = (lax.axis_size(axis), shard.shape[dim])
        up = [(i, (i + 1) % count) for i in range(count if wrap else count - 1)]
        down = [(j, i) for i, j in up]
        last = lax.slice_in_dim(shard, length - width, length, axis=dim)
        leading = lax.slice_in_dim(shard, 0, width, axis=dim)
        before = lax.ppermute(last, axis, up)
        after = lax.ppermute(leading, axis, down)
        shard = jnp.concatenate([before, shard, after], axis=dim)
    return shard


def rotate_rays(values, row_first, col_first, total_rows, total_cols):
    band_rows, sector_cols, feature_width = values.shape
    quarter = HD // 4
    head_count = feature_width // HD
    frequency = (jnp.arange(quarter, dtype=jnp.int32) + 1).astype(jnp.float32)
    row_ids = (row_first + jnp.arange(band_rows, dtype=jnp.int32)).astype(jnp.float32)
    col_ids = (col_first + jnp.arange(sector_cols, dtype=jnp.int32)).astype(jnp.float32)
    lat_angle = ((row_ids + 0.5) * (math.pi / total_rows))[:, None] * frequency[None, :]
    lon_angle = (col_ids * (2.0 * math.pi / total_cols))[:, None] * frequency[None, :]
    lat_cos = jnp.cos(lat_angle)[:, None, None, :]
    lat_sin = jnp.sin(lat_angle)[:, None, None, :]
    lon_cos = jnp.cos(lon_angle)[None, :, None, :]
    lon_sin = jnp.sin(lon_angle)[None, :, None, :]
    quarters = values.astype(jnp.float32).reshape(band_rows, sector_cols, head_count, 4, quarter)
    lat_one = quarters[:, :, :, 0, :]
    lat_two = quarters[:, :, :, 1, :]
    lon_one = quarters[:, :, :, 2, :]
    lon_two = quarters[:, :, :, 3, :]
    turned = jnp.stack(
        [
            lat_one * lat_cos - lat_two * lat_sin,
            lat_one * lat_sin + lat_two * lat_cos,
            lon_one * lon_cos - lon_two * lon_sin,
            lon_one * lon_sin + lon_two * lon_cos,
        ],
        axis=3,
    )
    return turned.reshape(band_rows, sector_cols, feature_width).astype(jnp.bfloat16)


def widen_rows(stacked, radius):
    padded = extended_2(stacked, (("lat", 1),), radius, False)
    return padded[:, : padded.shape[1] - 1]


def widen_cols(stacked, radius):
    padded = extended_2(stacked, (("lon", 2),), radius, True)
    return padded[:, :, : padded.shape[2] - 1]


def shards_halo(query_tok, key_tok, value_tok, query_tan, key_tan, value_tan):
    band_rows, sector_cols, feature_width = query_tok.shape
    radius = WIN // 2
    window_span = 2 * radius
    score_scale = 1.0 / math.sqrt(HD)
    total_rows = band_rows * lax.axis_size("lat")
    total_cols = sector_cols * lax.axis_size("lon")
    row_first = lax.axis_index("lat") * band_rows
    col_first = lax.axis_index("lon") * sector_cols
    rot_query = rotate_rays(query_tok, row_first, col_first, total_rows, total_cols)
    rot_qtan = rotate_rays(query_tan, row_first, col_first, total_rows, total_cols)
    rot_key = rotate_rays(key_tok, row_first, col_first, total_rows, total_cols)
    rot_ktan = rotate_rays(key_tan, row_first, col_first, total_rows, total_cols)
    stacked = jnp.stack([rot_key, rot_ktan, value_tok, value_tan])
    extended = widen_rows(widen_cols(stacked, radius), radius)
    ext_rows = band_rows + window_span - 1
    ext_cols = sector_cols + window_span - 1
    key_count = ext_rows * ext_cols
    query_count = band_rows * sector_cols
    keys_flat = extended.reshape(4, key_count, feature_width)
    query_flat = rot_query.reshape(query_count, feature_width)
    qtan_flat = rot_qtan.reshape(query_count, feature_width)
    key_ids = jnp.arange(key_count, dtype=jnp.int32)
    query_ids = jnp.arange(query_count, dtype=jnp.int32)
    row_gap = (key_ids // ext_cols)[None, :] - (query_ids // sector_cols)[:, None]
    col_gap = (key_ids % ext_cols)[None, :] - (query_ids % sector_cols)[:, None]
    key_rows = row_first - radius + key_ids // ext_cols
    allowed = (
        (row_gap >= 0)
        & (row_gap < window_span)
        & (col_gap >= 0)
        & (col_gap < window_span)
        & ((key_rows >= 0) & (key_rows < total_rows))[None, :]
    )
    head_count = feature_width // HD
    group_size = math.gcd(head_count, 4)
    out_groups = []
    tan_groups = []
    for group_index in range(head_count // group_size):
        low_col = group_index * group_size * HD
        high_col = low_col + group_size * HD
        q_part = query_flat[:, low_col:high_col].reshape(query_count, group_size, HD)
        qt_part = qtan_flat[:, low_col:high_col].reshape(query_count, group_size, HD)
        k_part = keys_flat[0][:, low_col:high_col].reshape(key_count, group_size, HD)
        kt_part = keys_flat[1][:, low_col:high_col].reshape(key_count, group_size, HD)
        v_part = keys_flat[2][:, low_col:high_col].reshape(key_count, group_size, HD)
        vt_part = keys_flat[3][:, low_col:high_col].reshape(key_count, group_size, HD)
        scores = (
            jnp.einsum("qhd,khd->hqk", q_part, k_part, preferred_element_type=jnp.float32)
            * score_scale
        )
        scores = jnp.where(allowed[None], scores, -1e30)
        row_top = jnp.max(scores, axis=-1, keepdims=True)
        exp_scores = jnp.exp(scores - row_top)
        attention = exp_scores / jnp.sum(exp_scores, axis=-1, keepdims=True)
        slopes = (
            jnp.einsum("qhd,khd->hqk", qt_part, k_part, preferred_element_type=jnp.float32)
            + jnp.einsum("qhd,khd->hqk", q_part, kt_part, preferred_element_type=jnp.float32)
        ) * score_scale
        mean_slope = jnp.sum(attention * slopes, axis=-1, keepdims=True)
        weight_b = (attention * (slopes - mean_slope)).astype(jnp.bfloat16)
        prob_b = attention.astype(jnp.bfloat16)
        group_out = jnp.einsum("hqk,khd->qhd", prob_b, v_part, preferred_element_type=jnp.float32)
        group_tan = jnp.einsum(
            "hqk,khd->qhd", weight_b, v_part, preferred_element_type=jnp.float32
        ) + jnp.einsum("hqk,khd->qhd", prob_b, vt_part, preferred_element_type=jnp.float32)
        out_groups.append(group_out.reshape(query_count, group_size * HD))
        tan_groups.append(group_tan.reshape(query_count, group_size * HD))
    attended = jnp.concatenate(out_groups, axis=1).astype(jnp.bfloat16)
    attended_tan = jnp.concatenate(tan_groups, axis=1).astype(jnp.bfloat16)
    return (
        attended.reshape(band_rows, sector_cols, feature_width),
        attended_tan.reshape(band_rows, sector_cols, feature_width),
    )


BF = jnp.bfloat16
F32 = jnp.float32
MESH = pl.DeviceIdType.MESH


def ray_tables(total_rows, total_cols):
    quarter = HD // 4
    freq = (np.arange(quarter) + 1).astype(np.float32)
    rows = np.arange(total_rows).astype(np.float32)
    cols = np.arange(total_cols).astype(np.float32)
    lat = ((rows + np.float32(0.5)) * np.float32(math.pi / total_rows))[:, None] * freq[None, :]
    lon = (cols * np.float32(2.0 * math.pi / total_cols))[:, None] * freq[None, :]

    def table(fn, angle, first):
        part = fn(angle.astype(np.float64)).astype(np.float32)
        none = np.zeros_like(part)
        return np.concatenate([part, part, none, none] if first else [none, none, part, part], axis=1)

    row_tab = np.stack([table(np.cos, lat, True), table(np.sin, lat, True)])
    col_tab = np.stack([table(np.cos, lon, False), table(np.sin, lon, False)])
    return row_tab, col_tab


def kernel(
    n, n_lon, hp, band,
    q_ref, k_ref, v_ref, qt_ref, kt_ref, vt_ref, row_hbm, col_hbm,
    both_ref,
    raw_kv, raw_q, kvb, hs, outs, turn, bias, row_tab, col_tab,
    kv_send, kv_recv, q_send, q_recv, h_send, h_recv, o_send, o_recv, t_loc, greet, near, peers,
):
    me = lax.axis_index("lat")
    lon = lax.axis_index("lon")
    left = lax.rem(lon + n_lon - 1, n_lon)
    right = lax.rem(lon + 1, n_lon)
    cols = 16
    total = n * band
    pairs = total // 2

    def told(sem, lat, sector):
        pl.semaphore_signal(sem, inc=1, device_id=(lat, sector), device_id_type=MESH)

    barrier = pltpu.get_barrier_semaphore()
    lead, late = me == 0, me == n - 1
    middle = jnp.logical_not(jnp.logical_or(lead, late))
    first, last = lon == 0, lon == n_lon - 1
    odd = lax.rem(lon, 2) == 1
    middle_odd = jnp.logical_and(odd, jnp.logical_not(last))
    middle_even = jnp.logical_and(jnp.logical_not(odd), jnp.logical_not(first))

    @pl.when(lead)
    def _():
        for d in range(1, n):
            told(barrier, d, lon)

    @pl.when(middle)
    def _():
        told(barrier, 0, lon)
        told(barrier, n - 1, lon)

    @pl.when(jnp.logical_and(lead, jnp.logical_or(odd, first)))
    def _():
        told(barrier, me, left)

    @pl.when(jnp.logical_and(lead, middle_odd))
    def _():
        told(barrier, me, right)

    kv_refs = (k_ref, kt_ref, v_ref, vt_ref)
    q_refs = (q_ref, qt_ref)
    parts = tuple((j, 1) for j in range(hp))
    order = (0, *range(n - 2, 0, -1), n - 1)

    def taken(ref, sem):
        pltpu.make_async_copy(ref, ref, sem).wait()

    def lanes(owner, j, count):
        return pl.ds(pl.multiple_of((owner * hp + j) * HD, HD), count * HD)

    def kv_copy(a, p, peer):
        j, count = parts[p]
        return pltpu.make_async_remote_copy(
            src_ref=kv_refs[a].at[:, :, lanes(peer, j, count)],
            dst_ref=raw_kv.at[a, pl.ds(me * band, band), :, j * HD:(j + count) * HD],
            send_sem=kv_send,
            recv_sem=kv_recv.at[p, a],
            device_id=(peer, lon),
            device_id_type=MESH,
        )

    def q_copy(a, j, peer):
        return pltpu.make_async_remote_copy(
            src_ref=q_refs[a].at[:, :, lanes(peer, j, 1)],
            dst_ref=raw_q.at[j, a, pl.ds(me * band, band)],
            send_sem=q_send,
            recv_sem=q_recv.at[j],
            device_id=(peer, lon),
            device_id_type=MESH,
        )

    def own_q(a, j):
        return pltpu.make_async_copy(
            q_refs[a].at[:, :, lanes(me, j, 1)],
            raw_q.at[j, a, pl.ds(me * band, band)],
            q_recv.at[j],
        )

    def own_copy(a, p):
        j, count = parts[p]
        return pltpu.make_async_copy(
            kv_refs[a].at[:, :, lanes(me, j, count)],
            raw_kv.at[a, pl.ds(me * band, band), :, j * HD:(j + count) * HD],
            kv_recv.at[p, a],
        )

    halos = [(p, slice(0, 4)) for p in range(hp - 1)] + [(hp - 1, slice(a, a + 1)) for a in range(4)]

    def halo_copy(side, h):
        p, arrays = halos[h]
        j, count = parts[p]
        return pltpu.make_async_remote_copy(
            src_ref=hs.at[side, arrays, j:j + count],
            dst_ref=kvb.at[arrays, j:j + count, :, 3 - side],
            send_sem=h_send,
            recv_sem=h_recv.at[p],
            device_id=(me, right if side else left),
            device_id_type=MESH,
        )

    def out_copy(j, d):
        peer = lax.rem(me + d, n)
        return pltpu.make_async_remote_copy(
            src_ref=outs.at[j, :, pl.ds(peer * band, band)],
            dst_ref=both_ref.at[:, :, :, lanes(me, j, 1)],
            send_sem=o_send,
            recv_sem=o_recv,
            device_id=(peer, lon),
            device_id_type=MESH,
        )

    def own_out(j):
        return pltpu.make_async_copy(
            outs.at[j, :, pl.ds(me * band, band)],
            both_ref.at[:, :, :, lanes(me, j, 1)],
            o_recv,
        )

    def send_out(j, b):
        @pl.when(me == b)
        def _():
            own_out(j).start()

        @pl.when(me != b)
        def _():
            out_copy(j, lax.rem(b - me + n, n)).start()

    here = pl.ds(pl.multiple_of(lon * cols, cols), cols)
    row_copy = pltpu.make_async_copy(row_hbm, row_tab, t_loc.at[0])
    col_copy = pltpu.make_async_copy(col_hbm.at[:, here], col_tab, t_loc.at[1])
    row_copy.start()
    col_copy.start()

    @pl.when(late)
    def _():
        pl.semaphore_wait(barrier, n - 1)
        for d in range(n - 1):
            told(peers, d, lon)

    @pl.when(middle)
    def _():
        pl.semaphore_wait(barrier, 1)

    @pl.when(jnp.logical_and(lead, middle_odd))
    def _():
        pl.semaphore_wait(barrier, n - 2)

    @pl.when(jnp.logical_and(lead, middle_even))
    def _():
        pl.semaphore_wait(barrier, n)

    @pl.when(jnp.logical_and(lead, jnp.logical_or(first, last)))
    def _():
        pl.semaphore_wait(barrier, n - 1)

    @pl.when(jnp.logical_not(lead))
    def _():
        for a in range(4):
            kv_copy(a, 0, 0).start()

    @pl.when(lead)
    def _():
        for d in range(1, n - 1):
            for a in range(4):
                kv_copy(a, 0, d).start()

    @pl.when(jnp.logical_not(late))
    def _():
        pl.semaphore_wait(peers, 1)

    @pl.when(jnp.logical_and(lead, middle_even))
    def _():
        told(near.at[1], me, left)
        told(near.at[0], me, right)

    @pl.when(jnp.logical_and(lead, jnp.logical_or(first, last)))
    def _():
        told(near.at[0], me, right)

    @pl.when(lead)
    def _():
        for a in range(4):
            kv_copy(a, 0, n - 1).start()

    for peer in order[1:]:
        @pl.when(jnp.logical_not(jnp.logical_or(lead, peer == me)))
        def _():
            for a in range(4):
                kv_copy(a, 0, peer).start()

    for a in range(4):
        own_copy(a, 0).start()
    for p in range(1, len(parts)):
        for peer in order:
            @pl.when(peer != me)
            def _():
                for a in range(4):
                    kv_copy(a, p, peer).start()

        for a in range(4):
            own_copy(a, p).start()
    for j in range(hp):
        for which, peers_in_turn in ((0, order), (1, (0, *range(1, n)))):
            for peer in peers_in_turn:
                @pl.when(jnp.logical_and(peer != me, lax.rem(lon, 2) == which))
                def _():
                    for a in range(2):
                        q_copy(a, j, peer).start()

        for a in range(2):
            own_q(a, j).start()

    row_copy.wait()
    col_copy.wait()
    for t in range(2):
        whole = row_tab[t][:, None, :] + col_tab[t][None, :, :]
        turn[t] = whole.reshape(total * cols, HD)
    shape = (band * cols, (band + WIN) * 2 * cols)
    query = lax.broadcasted_iota(jnp.int32, shape, 0)
    key = lax.broadcasted_iota(jnp.int32, shape, 1)
    part = (key % 64) // 16
    spot = key % 16
    own = part < 2
    key_row = (key // 64) * 2 + jnp.where(own, part, spot // 8)
    key_col = jnp.where(own, spot, jnp.where(part == 2, spot % 8 - 8, spot % 8 + 16))
    row_gap = key_row - query // 16
    col_gap = key_col - query % 16 + WIN // 2
    allowed = (row_gap >= 0) & (row_gap < WIN) & (col_gap >= 0) & (col_gap < WIN)
    bias[...] = jnp.where(allowed, 0.0, -1e30)
    src = lax.broadcasted_iota(jnp.int32, (HD, HD), 0)
    dst = lax.broadcasted_iota(jnp.int32, (HD, HD), 1)
    low = (dst % 64) < 32
    swap = (
        jnp.where(low & (src == dst + 32), -1.0, 0.0)
        + jnp.where(jnp.logical_not(low) & (src == dst - 32), 1.0, 0.0)
    ).astype(BF)

    def turned(x):
        flat = x.reshape(total * cols, HD)
        other = jnp.dot(flat, swap, preferred_element_type=F32)
        return flat.astype(F32) * turn[0] + other * turn[1]

    def stage(a, j):
        x = raw_kv[a, :, :, pl.ds(pl.multiple_of(j * HD, HD), HD)]
        y = turned(x) if a < 2 else x.reshape(total * cols, HD).astype(F32)
        kvb[a, j, :, 0:2] = y.reshape(pairs, 2, cols, HD).astype(BF)
        halves = y.reshape(total, 2, cols // 2, HD)
        for side in range(2):
            hs[side, a, j] = halves[:, side].reshape(pairs, cols, HD).astype(BF)

    @pl.when(lead)
    def _():
        pl.semaphore_wait(near.at[0], 1)

        @pl.when(jnp.logical_or(middle_odd, last))
        def _():
            told(near.at[1], me, left)

        pl.semaphore_wait(near.at[1], 1)

        @pl.when(middle_odd)
        def _():
            told(near.at[0], me, right)

        @pl.when(first)
        def _():
            told(near.at[1], me, left)

        for d in range(1, n):
            told(greet, lax.rem(me + d, n), lon)

    for p in range(len(parts)):
        for a in range(4):
            j, count = parts[p]
            taken(raw_kv.at[a, :, :, j * HD:(j + count) * HD], kv_recv.at[p, a])
            if parts[p][1] == 1:
                stage(a, parts[p][0])
            else:
                pl.loop(parts[p][0], sum(parts[p]))(functools.partial(stage, a))
            if p == 0 and a == 0:
                @pl.when(jnp.logical_not(lead))
                def _():
                    pl.semaphore_wait(greet, 1)

            for h in range(len(halos)):
                if halos[h][0] == p and halos[h][1].stop == a + 1:
                    for side in range(2):
                        halo_copy(side, h).start()

    scale2 = math.log2(math.e) / math.sqrt(HD)
    scale = 1.0 / math.sqrt(HD)

    @pl.loop(0, hp)
    def _(j):
        for p in range(len(parts)):
            @pl.when(j == parts[p][0])
            def _():
                taken(kvb.at[:, parts[p][0]:sum(parts[p]), :, 2:4], h_recv.at[p])

        taken(raw_q.at[j], q_recv.at[j])
        for a in range(2):
            raw_q[j, a] = turned(raw_q[j, a]).astype(BF).reshape(total, cols, HD)
        nq = band * cols
        for b in order:
            first = max(0, b * band - WIN // 2)
            last = min(total, (b + 1) * band + WIN // 2)
            skip = (first - (b * band - WIN // 2)) // 2 * 64
            p0, p1 = first // 2, last // 2
            nk = (p1 - p0) * 64
            keys = kvb[0, j, p0:p1].reshape(nk, HD)
            ktan = kvb[1, j, p0:p1].reshape(nk, HD)
            val = kvb[2, j, p0:p1].reshape(nk, HD)
            vtan = kvb[3, j, p0:p1].reshape(nk, HD)
            rows = slice(b * band, (b + 1) * band)
            q = raw_q[j, 0, rows].reshape(nq, HD)
            qt = raw_q[j, 1, rows].reshape(nq, HD)
            nt = (((1,), (1,)), ((), ()))
            score = lax.dot_general(q, keys, nt, preferred_element_type=F32)
            score = score * scale2 + bias[:, skip:skip + nk]
            top = jnp.max(score, axis=-1, keepdims=True)
            e = jnp.exp2(score - top)
            inv = 1.0 / jnp.sum(e, axis=-1, keepdims=True)
            slope = lax.dot_general(
                jnp.concatenate([qt, q], axis=1),
                jnp.concatenate([keys, ktan], axis=1),
                nt,
                preferred_element_type=F32,
            )
            mean = jnp.sum(e * slope, axis=-1, keepdims=True) * inv
            prob = e * inv
            prob_b = prob.astype(BF)
            weight_b = (prob * ((slope - mean) * scale)).astype(BF)
            both = jnp.dot(
                prob_b, jnp.concatenate([val, vtan], axis=1), preferred_element_type=F32
            )
            tan = both[:, HD:] + jnp.dot(weight_b, val, preferred_element_type=F32)
            outs[j, 0, rows] = both[:, :HD].astype(BF).reshape(band, cols, HD)
            outs[j, 1, rows] = tan.astype(BF).reshape(band, cols, HD)

            @pl.when(jnp.logical_not(odd))
            def _():
                send_out(j, b)

        @pl.when(odd)
        def _():
            for b in order:
                send_out(j, b)

    taken(raw_kv.at[:, 0:total - band], kv_send)
    taken(raw_q.at[:, :, 0:total - band], q_send)
    taken(hs, h_send)
    taken(outs.at[:, :, 0:total - band], o_send)
    taken(both_ref, o_recv)


def spread(both_ref, out_ref, tan_ref, sems):
    copies = [
        pltpu.make_async_copy(both_ref.at[o], ref, sems.at[o])
        for o, ref in enumerate((out_ref, tan_ref))
    ]
    for copy in copies:
        copy.start()
    for copy in copies:
        copy.wait()


def shards(mesh_shape, *args):
    band, cols, width = args[0].shape
    n, n_lon = mesh_shape["lat"], mesh_shape["lon"]
    heads = width // HD
    fits = (
        heads % n == 0 and n > 1 and n_lon > 2 and n_lon % 2 == 0
        and cols == WIN and band == WIN // 2
    )
    if not fits:
        return shards_halo(*args)
    hp = heads // n
    total = band * n
    row_tab, col_tab = ray_tables(total, cols * n_lon)
    hbm = pl.BlockSpec(memory_space=pltpu.HBM)
    anywhere = pl.BlockSpec(memory_space=pl.ANY)
    q, k, v, qt, kt, vt = args
    dma = pltpu.SemaphoreType.DMA
    nq = band * cols
    nk = (band + WIN) * 2 * cols
    both = pl.pallas_call(
        functools.partial(kernel, n, n_lon, hp, band),
        out_shape=pltpu.VMEM((2, band, cols, width), BF),
        in_specs=[hbm] * 8,
        out_specs=anywhere,
        scratch_shapes=[
            pltpu.VMEM((4, total, cols, hp * HD), BF),
            pltpu.VMEM((hp, 2, total, cols, HD), BF),
            pltpu.VMEM((4, hp, total // 2, 4, cols, HD), BF),
            pltpu.VMEM((2, 4, hp, total // 2, cols, HD), BF),
            pltpu.VMEM((hp, 2, total, cols, HD), BF),
            pltpu.VMEM((2, total * cols, HD), F32),
            pltpu.VMEM((nq, nk), F32),
            pltpu.VMEM((2, total, HD), F32),
            pltpu.VMEM((2, cols, HD), F32),
            dma,
            dma((hp, 4)),
            dma,
            dma((hp,)),
            dma,
            dma((hp,)),
            dma,
            dma,
            dma((2,)),
            pltpu.SemaphoreType.REGULAR,
            pltpu.SemaphoreType.REGULAR((2,)),
            pltpu.SemaphoreType.REGULAR,
        ],
        compiler_params=pltpu.CompilerParams(
            collective_id=0, has_side_effects=True, vmem_limit_bytes=60 * 1024 * 1024
        ),
        name="panorama",
    )(q, k, v, qt, kt, vt, jnp.asarray(row_tab), jnp.asarray(col_tab))
    return tuple(
        pl.pallas_call(
            spread,
            out_shape=[jax.ShapeDtypeStruct((band, cols, width), BF)] * 2,
            in_specs=[anywhere],
            out_specs=[hbm] * 2,
            scratch_shapes=[dma((2,))],
            name="spread",
        )(pltpu.with_memory_space_constraint(both, pltpu.VMEM))
    )


def solution(mesh):
    placed = (
        P("lat", "lon", None),
        P("lat", "lon", None),
        P("lat", "lon", None),
        P("lat", "lon", None),
        P("lat", "lon", None),
        P("lat", "lon", None),
    )
    return jax.shard_map(
        functools.partial(shards, dict(mesh.shape)),
        mesh=mesh,
        in_specs=placed,
        out_specs=(P("lat", "lon", None), P("lat", "lon", None)),
        check_vma=False,
    )
```

```python
import functools
import math

import jax
import jax.numpy as jnp
import numpy as np
from jax import lax
from jax.experimental import pallas as pl
from jax.experimental.pallas import tpu as pltpu
from jax.sharding import PartitionSpec as P

HD = 128
WIN = 16


def extended_2(shard, sides, width, wrap):
    for axis, dim in sides:
        count, length = (lax.axis_size(axis), shard.shape[dim])
        up = [(i, (i + 1) % count) for i in range(count if wrap else count - 1)]
        down = [(j, i) for i, j in up]
        last = lax.slice_in_dim(shard, length - width, length, axis=dim)
        leading = lax.slice_in_dim(shard, 0, width, axis=dim)
        before = lax.ppermute(last, axis, up)
        after = lax.ppermute(leading, axis, down)
        shard = jnp.concatenate([before, shard, after], axis=dim)
    return shard


def rotate_rays(values, row_first, col_first, total_rows, total_cols):
    band_rows, sector_cols, feature_width = values.shape
    quarter = HD // 4
    head_count = feature_width // HD
    frequency = (jnp.arange(quarter, dtype=jnp.int32) + 1).astype(jnp.float32)
    row_ids = (row_first + jnp.arange(band_rows, dtype=jnp.int32)).astype(jnp.float32)
    col_ids = (col_first + jnp.arange(sector_cols, dtype=jnp.int32)).astype(jnp.float32)
    lat_angle = ((row_ids + 0.5) * (math.pi / total_rows))[:, None] * frequency[None, :]
    lon_angle = (col_ids * (2.0 * math.pi / total_cols))[:, None] * frequency[None, :]
    lat_cos = jnp.cos(lat_angle)[:, None, None, :]
    lat_sin = jnp.sin(lat_angle)[:, None, None, :]
    lon_cos = jnp.cos(lon_angle)[None, :, None, :]
    lon_sin = jnp.sin(lon_angle)[None, :, None, :]
    quarters = values.astype(jnp.float32).reshape(band_rows, sector_cols, head_count, 4, quarter)
    lat_one = quarters[:, :, :, 0, :]
    lat_two = quarters[:, :, :, 1, :]
    lon_one = quarters[:, :, :, 2, :]
    lon_two = quarters[:, :, :, 3, :]
    turned = jnp.stack(
        [
            lat_one * lat_cos - lat_two * lat_sin,
            lat_one * lat_sin + lat_two * lat_cos,
            lon_one * lon_cos - lon_two * lon_sin,
            lon_one * lon_sin + lon_two * lon_cos,
        ],
        axis=3,
    )
    return turned.reshape(band_rows, sector_cols, feature_width).astype(jnp.bfloat16)


def widen_rows(stacked, radius):
    padded = extended_2(stacked, (("lat", 1),), radius, False)
    return padded[:, : padded.shape[1] - 1]


def widen_cols(stacked, radius):
    padded = extended_2(stacked, (("lon", 2),), radius, True)
    return padded[:, :, : padded.shape[2] - 1]


def shards_halo(query_tok, key_tok, value_tok, query_tan, key_tan, value_tan):
    band_rows, sector_cols, feature_width = query_tok.shape
    radius = WIN // 2
    window_span = 2 * radius
    score_scale = 1.0 / math.sqrt(HD)
    total_rows = band_rows * lax.axis_size("lat")
    total_cols = sector_cols * lax.axis_size("lon")
    row_first = lax.axis_index("lat") * band_rows
    col_first = lax.axis_index("lon") * sector_cols
    rot_query = rotate_rays(query_tok, row_first, col_first, total_rows, total_cols)
    rot_qtan = rotate_rays(query_tan, row_first, col_first, total_rows, total_cols)
    rot_key = rotate_rays(key_tok, row_first, col_first, total_rows, total_cols)
    rot_ktan = rotate_rays(key_tan, row_first, col_first, total_rows, total_cols)
    stacked = jnp.stack([rot_key, rot_ktan, value_tok, value_tan])
    extended = widen_rows(widen_cols(stacked, radius), radius)
    ext_rows = band_rows + window_span - 1
    ext_cols = sector_cols + window_span - 1
    key_count = ext_rows * ext_cols
    query_count = band_rows * sector_cols
    keys_flat = extended.reshape(4, key_count, feature_width)
    query_flat = rot_query.reshape(query_count, feature_width)
    qtan_flat = rot_qtan.reshape(query_count, feature_width)
    key_ids = jnp.arange(key_count, dtype=jnp.int32)
    query_ids = jnp.arange(query_count, dtype=jnp.int32)
    row_gap = (key_ids // ext_cols)[None, :] - (query_ids // sector_cols)[:, None]
    col_gap = (key_ids % ext_cols)[None, :] - (query_ids % sector_cols)[:, None]
    key_rows = row_first - radius + key_ids // ext_cols
    allowed = (
        (row_gap >= 0)
        & (row_gap < window_span)
        & (col_gap >= 0)
        & (col_gap < window_span)
        & ((key_rows >= 0) & (key_rows < total_rows))[None, :]
    )
    head_count = feature_width // HD
    group_size = math.gcd(head_count, 4)
    out_groups = []
    tan_groups = []
    for group_index in range(head_count // group_size):
        low_col = group_index * group_size * HD
        high_col = low_col + group_size * HD
        q_part = query_flat[:, low_col:high_col].reshape(query_count, group_size, HD)
        qt_part = qtan_flat[:, low_col:high_col].reshape(query_count, group_size, HD)
        k_part = keys_flat[0][:, low_col:high_col].reshape(key_count, group_size, HD)
        kt_part = keys_flat[1][:, low_col:high_col].reshape(key_count, group_size, HD)
        v_part = keys_flat[2][:, low_col:high_col].reshape(key_count, group_size, HD)
        vt_part = keys_flat[3][:, low_col:high_col].reshape(key_count, group_size, HD)
        scores = (
            jnp.einsum("qhd,khd->hqk", q_part, k_part, preferred_element_type=jnp.float32)
            * score_scale
        )
        scores = jnp.where(allowed[None], scores, -1e30)
        row_top = jnp.max(scores, axis=-1, keepdims=True)
        exp_scores = jnp.exp(scores - row_top)
        attention = exp_scores / jnp.sum(exp_scores, axis=-1, keepdims=True)
        slopes = (
            jnp.einsum("qhd,khd->hqk", qt_part, k_part, preferred_element_type=jnp.float32)
            + jnp.einsum("qhd,khd->hqk", q_part, kt_part, preferred_element_type=jnp.float32)
        ) * score_scale
        mean_slope = jnp.sum(attention * slopes, axis=-1, keepdims=True)
        weight_b = (attention * (slopes - mean_slope)).astype(jnp.bfloat16)
        prob_b = attention.astype(jnp.bfloat16)
        group_out = jnp.einsum("hqk,khd->qhd", prob_b, v_part, preferred_element_type=jnp.float32)
        group_tan = jnp.einsum(
            "hqk,khd->qhd", weight_b, v_part, preferred_element_type=jnp.float32
        ) + jnp.einsum("hqk,khd->qhd", prob_b, vt_part, preferred_element_type=jnp.float32)
        out_groups.append(group_out.reshape(query_count, group_size * HD))
        tan_groups.append(group_tan.reshape(query_count, group_size * HD))
    attended = jnp.concatenate(out_groups, axis=1).astype(jnp.bfloat16)
    attended_tan = jnp.concatenate(tan_groups, axis=1).astype(jnp.bfloat16)
    return (
        attended.reshape(band_rows, sector_cols, feature_width),
        attended_tan.reshape(band_rows, sector_cols, feature_width),
    )


BF = jnp.bfloat16
F32 = jnp.float32
MESH = pl.DeviceIdType.MESH


def ray_tables(total_rows, total_cols):
    quarter = HD // 4
    freq = (np.arange(quarter) + 1).astype(np.float32)
    rows = np.arange(total_rows).astype(np.float32)
    cols = np.arange(total_cols).astype(np.float32)
    lat = ((rows + np.float32(0.5)) * np.float32(math.pi / total_rows))[:, None] * freq[None, :]
    lon = (cols * np.float32(2.0 * math.pi / total_cols))[:, None] * freq[None, :]

    def table(fn, angle, first):
        part = fn(angle.astype(np.float64)).astype(np.float32)
        none = np.zeros_like(part)
        return np.concatenate([part, part, none, none] if first else [none, none, part, part], axis=1)

    row_tab = np.stack([table(np.cos, lat, True), table(np.sin, lat, True)])
    col_tab = np.stack([table(np.cos, lon, False), table(np.sin, lon, False)])
    return row_tab, col_tab


def kernel(
    n, n_lon, hp, band,
    q_ref, k_ref, v_ref, qt_ref, kt_ref, vt_ref, row_hbm, col_hbm,
    both_ref,
    raw_kv, raw_q, kvb, hs, outs, turn, bias, row_tab, col_tab,
    kv_send, kv_recv, q_send, q_recv, h_send, h_recv, o_send, o_recv, t_loc, greet, near, peers,
):
    me = lax.axis_index("lat")
    lon = lax.axis_index("lon")
    left = lax.rem(lon + n_lon - 1, n_lon)
    right = lax.rem(lon + 1, n_lon)
    cols = 16
    total = n * band
    pairs = total // 2

    def told(sem, lat, sector):
        pl.semaphore_signal(sem, inc=1, device_id=(lat, sector), device_id_type=MESH)

    barrier = pltpu.get_barrier_semaphore()
    lead, late = me == 0, me == n - 1
    middle = jnp.logical_not(jnp.logical_or(lead, late))
    first, last = lon == 0, lon == n_lon - 1
    odd = lax.rem(lon, 2) == 1
    middle_odd = jnp.logical_and(odd, jnp.logical_not(last))
    middle_even = jnp.logical_and(jnp.logical_not(odd), jnp.logical_not(first))

    @pl.when(lead)
    def _():
        for d in range(1, n):
            told(barrier, d, lon)

    @pl.when(middle)
    def _():
        told(barrier, 0, lon)
        told(barrier, n - 1, lon)

    @pl.when(jnp.logical_and(lead, jnp.logical_or(odd, first)))
    def _():
        told(barrier, me, left)

    @pl.when(jnp.logical_and(lead, middle_odd))
    def _():
        told(barrier, me, right)

    kv_refs = (k_ref, kt_ref, v_ref, vt_ref)
    q_refs = (q_ref, qt_ref)
    parts = tuple((j, 1) for j in range(hp))
    order = (0, *range(n - 2, 0, -1), n - 1)

    def taken(ref, sem):
        pltpu.make_async_copy(ref, ref, sem).wait()

    def lanes(owner, j, count):
        return pl.ds(pl.multiple_of((owner * hp + j) * HD, HD), count * HD)

    def kv_copy(a, p, peer):
        j, count = parts[p]
        return pltpu.make_async_remote_copy(
            src_ref=kv_refs[a].at[:, :, lanes(peer, j, count)],
            dst_ref=raw_kv.at[a, pl.ds(me * band, band), :, j * HD:(j + count) * HD],
            send_sem=kv_send,
            recv_sem=kv_recv.at[p if p < hp - 1 else p + a],
            device_id=(peer, lon),
            device_id_type=MESH,
        )

    def q_copy(a, j, peer):
        return pltpu.make_async_remote_copy(
            src_ref=q_refs[a].at[:, :, lanes(peer, j, 1)],
            dst_ref=raw_q.at[j, a, pl.ds(me * band, band)],
            send_sem=q_send,
            recv_sem=q_recv.at[j],
            device_id=(peer, lon),
            device_id_type=MESH,
        )

    def own_q(a, j):
        return pltpu.make_async_copy(
            q_refs[a].at[:, :, lanes(me, j, 1)],
            raw_q.at[j, a, pl.ds(me * band, band)],
            q_recv.at[j],
        )

    def own_copy(a, p):
        j, count = parts[p]
        return pltpu.make_async_copy(
            kv_refs[a].at[:, :, lanes(me, j, count)],
            raw_kv.at[a, pl.ds(me * band, band), :, j * HD:(j + count) * HD],
            kv_recv.at[p if p < hp - 1 else p + a],
        )

    halos = [(p, slice(0, 4)) for p in range(hp - 1)] + [(hp - 1, slice(a, a + 1)) for a in range(4)]

    def halo_copy(side, h):
        p, arrays = halos[h]
        j, count = parts[p]
        return pltpu.make_async_remote_copy(
            src_ref=hs.at[side, arrays, j:j + count],
            dst_ref=kvb.at[arrays, j:j + count, :, 3 - side],
            send_sem=h_send,
            recv_sem=h_recv.at[p],
            device_id=(me, right if side else left),
            device_id_type=MESH,
        )

    def out_copy(j, d):
        peer = lax.rem(me + d, n)
        return pltpu.make_async_remote_copy(
            src_ref=outs.at[j, :, pl.ds(peer * band, band)],
            dst_ref=both_ref.at[:, :, :, lanes(me, j, 1)],
            send_sem=o_send,
            recv_sem=o_recv,
            device_id=(peer, lon),
            device_id_type=MESH,
        )

    def own_out(j):
        return pltpu.make_async_copy(
            outs.at[j, :, pl.ds(me * band, band)],
            both_ref.at[:, :, :, lanes(me, j, 1)],
            o_recv,
        )

    def send_out(j, b):
        @pl.when(me == b)
        def _():
            own_out(j).start()

        @pl.when(me != b)
        def _():
            out_copy(j, lax.rem(b - me + n, n)).start()

    here = pl.ds(pl.multiple_of(lon * cols, cols), cols)
    row_copy = pltpu.make_async_copy(row_hbm, row_tab, t_loc.at[0])
    col_copy = pltpu.make_async_copy(col_hbm.at[:, here], col_tab, t_loc.at[1])
    row_copy.start()
    col_copy.start()

    @pl.when(late)
    def _():
        pl.semaphore_wait(barrier, n - 1)
        for d in range(n - 1):
            told(peers, d, lon)

    @pl.when(middle)
    def _():
        pl.semaphore_wait(barrier, 1)

    @pl.when(jnp.logical_and(lead, middle_odd))
    def _():
        pl.semaphore_wait(barrier, n - 2)

    @pl.when(jnp.logical_and(lead, middle_even))
    def _():
        pl.semaphore_wait(barrier, n)

    @pl.when(jnp.logical_and(lead, jnp.logical_or(first, last)))
    def _():
        pl.semaphore_wait(barrier, n - 1)

    @pl.when(jnp.logical_not(lead))
    def _():
        for a in range(4):
            kv_copy(a, 0, 0).start()

    @pl.when(lead)
    def _():
        for d in range(1, n - 1):
            for a in range(4):
                kv_copy(a, 0, d).start()

    @pl.when(jnp.logical_not(late))
    def _():
        pl.semaphore_wait(peers, 1)

    @pl.when(jnp.logical_and(lead, middle_even))
    def _():
        told(near.at[1], me, left)
        told(near.at[0], me, right)

    @pl.when(jnp.logical_and(lead, jnp.logical_or(first, last)))
    def _():
        told(near.at[0], me, right)

    @pl.when(lead)
    def _():
        for a in range(4):
            kv_copy(a, 0, n - 1).start()

    for peer in order[1:]:
        @pl.when(jnp.logical_not(jnp.logical_or(lead, peer == me)))
        def _():
            for a in range(4):
                kv_copy(a, 0, peer).start()

    for a in range(4):
        own_copy(a, 0).start()
    for p in range(1, len(parts)):
        for peer in order:
            @pl.when(peer != me)
            def _():
                for a in range(4):
                    kv_copy(a, p, peer).start()

        for a in range(4):
            own_copy(a, p).start()
    for j in range(hp):
        for peer in order:
            @pl.when(peer != me)
            def _():
                for a in range(2):
                    q_copy(a, j, peer).start()

        for a in range(2):
            own_q(a, j).start()

    row_copy.wait()
    col_copy.wait()
    for t in range(2):
        whole = row_tab[t][:, None, :] + col_tab[t][None, :, :]
        turn[t] = whole.reshape(total * cols, HD)
    shape = (band * cols, (band + WIN) * 2 * cols)
    query = lax.broadcasted_iota(jnp.int32, shape, 0)
    key = lax.broadcasted_iota(jnp.int32, shape, 1)
    part = (key % 64) // 16
    spot = key % 16
    own = part < 2
    key_row = (key // 64) * 2 + jnp.where(own, part, spot // 8)
    key_col = jnp.where(own, spot, jnp.where(part == 2, spot % 8 - 8, spot % 8 + 16))
    row_gap = key_row - query // 16
    col_gap = key_col - query % 16 + WIN // 2
    allowed = (row_gap >= 0) & (row_gap < WIN) & (col_gap >= 0) & (col_gap < WIN)
    bias[...] = jnp.where(allowed, 0.0, -1e30)
    src = lax.broadcasted_iota(jnp.int32, (HD, HD), 0)
    dst = lax.broadcasted_iota(jnp.int32, (HD, HD), 1)
    low = (dst % 64) < 32
    swap = (
        jnp.where(low & (src == dst + 32), -1.0, 0.0)
        + jnp.where(jnp.logical_not(low) & (src == dst - 32), 1.0, 0.0)
    ).astype(BF)

    def turned(x):
        flat = x.reshape(total * cols, HD)
        other = jnp.dot(flat, swap, preferred_element_type=F32)
        return flat.astype(F32) * turn[0] + other * turn[1]

    def stage(a, j):
        x = raw_kv[a, :, :, pl.ds(pl.multiple_of(j * HD, HD), HD)]
        y = turned(x) if a < 2 else x.reshape(total * cols, HD).astype(F32)
        kvb[a, j, :, 0:2] = y.reshape(pairs, 2, cols, HD).astype(BF)
        halves = y.reshape(total, 2, cols // 2, HD)
        for side in range(2):
            hs[side, a, j] = halves[:, side].reshape(pairs, cols, HD).astype(BF)

    @pl.when(lead)
    def _():
        pl.semaphore_wait(near.at[0], 1)

        @pl.when(jnp.logical_or(middle_odd, last))
        def _():
            told(near.at[1], me, left)

        pl.semaphore_wait(near.at[1], 1)

        @pl.when(middle_odd)
        def _():
            told(near.at[0], me, right)

        @pl.when(first)
        def _():
            told(near.at[1], me, left)

        for d in range(1, n):
            told(greet, lax.rem(me + d, n), lon)

    for p in range(len(parts)):
        for a in range(4):
            j, count = parts[p]
            if p == hp - 1:
                taken(raw_kv.at[a, :, :, j * HD:(j + count) * HD], kv_recv.at[p + a])
            elif a == 0:
                taken(raw_kv.at[:, :, :, j * HD:(j + count) * HD], kv_recv.at[p])
            if parts[p][1] == 1:
                stage(a, parts[p][0])
            else:
                pl.loop(parts[p][0], sum(parts[p]))(functools.partial(stage, a))
            if p == 0 and a == 0:
                @pl.when(jnp.logical_not(lead))
                def _():
                    pl.semaphore_wait(greet, 1)

            for h in range(len(halos)):
                if halos[h][0] == p and halos[h][1].stop == a + 1:
                    for side in range(2):
                        halo_copy(side, h).start()

    scale2 = math.log2(math.e) / math.sqrt(HD)
    scale = 1.0 / math.sqrt(HD)

    @pl.loop(0, hp)
    def _(j):
        for p in range(len(parts)):
            @pl.when(j == parts[p][0])
            def _():
                taken(kvb.at[:, parts[p][0]:sum(parts[p]), :, 2:4], h_recv.at[p])

        taken(raw_q.at[j], q_recv.at[j])
        for a in range(2):
            raw_q[j, a] = turned(raw_q[j, a]).astype(BF).reshape(total, cols, HD)
        nq = band * cols
        held = jnp.logical_and(jnp.logical_and(odd, j == hp - 1), jnp.logical_not(lead))
        for b in order:
            first = max(0, b * band - WIN // 2)
            last = min(total, (b + 1) * band + WIN // 2)
            skip = (first - (b * band - WIN // 2)) // 2 * 64
            p0, p1 = first // 2, last // 2
            nk = (p1 - p0) * 64
            keys = kvb[0, j, p0:p1].reshape(nk, HD)
            ktan = kvb[1, j, p0:p1].reshape(nk, HD)
            val = kvb[2, j, p0:p1].reshape(nk, HD)
            vtan = kvb[3, j, p0:p1].reshape(nk, HD)
            rows = slice(b * band, (b + 1) * band)
            q = raw_q[j, 0, rows].reshape(nq, HD)
            qt = raw_q[j, 1, rows].reshape(nq, HD)
            nt = (((1,), (1,)), ((), ()))
            score = lax.dot_general(q, keys, nt, preferred_element_type=F32)
            score = score * scale2 + bias[:, skip:skip + nk]
            top = jnp.max(score, axis=-1, keepdims=True)
            e = jnp.exp2(score - top)
            inv = 1.0 / jnp.sum(e, axis=-1, keepdims=True)
            slope = lax.dot_general(
                jnp.concatenate([qt, q], axis=1),
                jnp.concatenate([keys, ktan], axis=1),
                nt,
                preferred_element_type=F32,
            )
            mean = jnp.sum(e * slope, axis=-1, keepdims=True) * inv
            prob = e * inv
            prob_b = prob.astype(BF)
            weight_b = (prob * ((slope - mean) * scale)).astype(BF)
            both = jnp.dot(
                prob_b, jnp.concatenate([val, vtan], axis=1), preferred_element_type=F32
            )
            tan = both[:, HD:] + jnp.dot(weight_b, val, preferred_element_type=F32)
            outs[j, 0, rows] = both[:, :HD].astype(BF).reshape(band, cols, HD)
            outs[j, 1, rows] = tan.astype(BF).reshape(band, cols, HD)

            @pl.when(jnp.logical_not(held))
            def _():
                send_out(j, b)

        @pl.when(held)
        def _():
            for b in order:
                send_out(j, b)

    taken(raw_kv.at[:, 0:total - band], kv_send)
    taken(raw_q.at[:, :, 0:total - band], q_send)
    taken(hs, h_send)
    taken(outs.at[:, :, 0:total - band], o_send)
    taken(both_ref, o_recv)


def spread(both_ref, out_ref, tan_ref, sems):
    copies = [
        pltpu.make_async_copy(both_ref.at[o], ref, sems.at[o])
        for o, ref in enumerate((out_ref, tan_ref))
    ]
    for copy in copies:
        copy.start()
    for copy in copies:
        copy.wait()


def shards(mesh_shape, *args):
    band, cols, width = args[0].shape
    n, n_lon = mesh_shape["lat"], mesh_shape["lon"]
    heads = width // HD
    fits = (
        heads % n == 0 and n > 1 and n_lon > 2 and n_lon % 2 == 0
        and cols == WIN and band == WIN // 2
    )
    if not fits:
        return shards_halo(*args)
    hp = heads // n
    total = band * n
    row_tab, col_tab = ray_tables(total, cols * n_lon)
    hbm = pl.BlockSpec(memory_space=pltpu.HBM)
    anywhere = pl.BlockSpec(memory_space=pl.ANY)
    q, k, v, qt, kt, vt = args
    dma = pltpu.SemaphoreType.DMA
    nq = band * cols
    nk = (band + WIN) * 2 * cols
    both = pl.pallas_call(
        functools.partial(kernel, n, n_lon, hp, band),
        out_shape=pltpu.VMEM((2, band, cols, width), BF),
        in_specs=[hbm] * 8,
        out_specs=anywhere,
        scratch_shapes=[
            pltpu.VMEM((4, total, cols, hp * HD), BF),
            pltpu.VMEM((hp, 2, total, cols, HD), BF),
            pltpu.VMEM((4, hp, total // 2, 4, cols, HD), BF),
            pltpu.VMEM((2, 4, hp, total // 2, cols, HD), BF),
            pltpu.VMEM((hp, 2, total, cols, HD), BF),
            pltpu.VMEM((2, total * cols, HD), F32),
            pltpu.VMEM((nq, nk), F32),
            pltpu.VMEM((2, total, HD), F32),
            pltpu.VMEM((2, cols, HD), F32),
            dma,
            dma((hp + 3,)),
            dma,
            dma((hp,)),
            dma,
            dma((hp,)),
            dma,
            dma,
            dma((2,)),
            pltpu.SemaphoreType.REGULAR,
            pltpu.SemaphoreType.REGULAR((2,)),
            pltpu.SemaphoreType.REGULAR,
        ],
        compiler_params=pltpu.CompilerParams(
            collective_id=0, has_side_effects=True, vmem_limit_bytes=60 * 1024 * 1024
        ),
        name="panorama",
    )(q, k, v, qt, kt, vt, jnp.asarray(row_tab), jnp.asarray(col_tab))
    return tuple(
        pl.pallas_call(
            spread,
            out_shape=[jax.ShapeDtypeStruct((band, cols, width), BF)] * 2,
            in_specs=[anywhere],
            out_specs=[hbm] * 2,
            scratch_shapes=[dma((2,))],
            name="spread",
        )(pltpu.with_memory_space_constraint(both, pltpu.VMEM))
    )


def solution(mesh):
    placed = (
        P("lat", "lon", None),
        P("lat", "lon", None),
        P("lat", "lon", None),
        P("lat", "lon", None),
        P("lat", "lon", None),
        P("lat", "lon", None),
    )
    return jax.shard_map(
        functools.partial(shards, dict(mesh.shape)),
        mesh=mesh,
        in_specs=placed,
        out_specs=(P("lat", "lon", None), P("lat", "lon", None)),
        check_vma=False,
    )
```
